32 devices in a mesh: pair: 2 (over core), virt: 4 (over y, x), integ: 4 (over z).
Axes of the slice: x: 2, y: 2, z: 4, core: 2. Of those that a mesh axis runs over, the one named last changes fastest.
Arguments:
- amplitudes: bfloat16 [2, 4, 256, 256], P('pair', 'integ', 'virt'), may hold values from -4 to 4
- vv_factors: bfloat16 [64, 256, 256], P('integ'), may hold values from -0.25 to 0.25
- ov_factors: bfloat16 [64, 4, 256], P(None, 'integ'), may hold values from -0.75 to 0.75
- occ_energy_i: float32 [2], P('pair'), may hold values from -2 to -0.5
- occ_energy_j: float32 [4], P('integ'), may hold values from -2 to -0.5
- virt_energy: float32 [256], replicated, may hold values from 0.2 to 3
- vv_mask: int32 [2, 2], replicated, may hold values 0 or 1
- pair_domain: int32 [2, 4, 2], P('pair', 'integ'), may hold values 0 or 1
Outputs:
- update: bfloat16 [2, 4, 256, 256], P('pair', 'integ', 'virt')
The draws below stay inside these ranges and needn't reach their ends.
All inputs are finite; a program needn't handle non-finite values. No bound on the sum of `pair_domain` on one device may be relied on, other than what follows from the above.
Results may differ from the reference program's by a relative error of at most 0.014.
Values may be sent and summed in bfloat16 or wider, within the bound.
A program may use at most 64 MiB of HBM per device.

```python
import jax
import jax.numpy as jnp
from jax import lax

TILE_SIZE = 128
TILES = 2
AUX_DEV = 16
VIRTUALS = 256
AUXILIARY = 64
OCC_OWNED = 2
OCC_SLAB = 4


def plant(result, own_key, smallest, largest):
    place = [jax.random.randint(jax.random.fold_in(own_key, axis), (), 0, length) for axis, length in enumerate(result.shape)]
    widest = result.shape.index(max(result.shape))
    beside = place[:widest] + [(place[widest] + 1) % result.shape[widest]] + place[widest + 1:]
    return result.at[tuple(place)].set(smallest).at[tuple(beside)].set(largest)


def block_levels(rng, dims, split, least, largest):
    factor_of, own = 1.0, jax.random.fold_in(rng, 6)
    for dim, shards_of in split:
        draws = jnp.exp(jax.random.uniform(jax.random.fold_in(own, dim), (shards_of,), jnp.float32, least / len(split), largest / len(split)))
        factor_of = factor_of * jnp.repeat(draws, dims[dim] // shards_of).reshape([-1 if axis == dim else 1 for axis in range(len(dims))])
    return factor_of


def normal_values(own_key, shape, scale, reach, split=(), kind=jnp.bfloat16):
    values = jax.random.normal(own_key, shape, jnp.float32) * scale
    if len(split) > 0:
        values = block_levels(own_key, shape, split, -0.22, 0.18) * values
    return jnp.clip(values, min=-reach, max=reach).astype(kind)


def setup_inputs(seed: int = 0) -> dict:
    splits = jax.random.split(jax.random.key(seed), 9)
    amplitudes = normal_values(splits[0], (OCC_OWNED, OCC_SLAB, VIRTUALS, VIRTUALS), 0.5, 4.0, ((0, 2), (1, 4), (2, 4)))
    vv_factors = normal_values(splits[1], (AUXILIARY, VIRTUALS, VIRTUALS), (VIRTUALS * max(1, AUX_DEV // 6)) ** -0.5, 0.25, ((0, 4),))
    ov_factors = normal_values(splits[2], (AUXILIARY, OCC_SLAB, VIRTUALS), (VIRTUALS // 4) ** -0.5, 0.75, ((1, 4),))
    occ_energy_i = jnp.clip(-2.0 + 1.5 * jax.random.uniform(splits[3], (OCC_OWNED,), jnp.float32) ** block_levels(splits[3], (OCC_OWNED,), ((0, 2),), -0.2, 0.2), -2.0, -0.5)
    occ_energy_j = jnp.clip(-2.0 + 1.5 * jax.random.uniform(splits[4], (OCC_SLAB,), jnp.float32) ** block_levels(splits[4], (OCC_SLAB,), ((0, 4),), -0.2, 0.2), -2.0, -0.5)
    virt_energy = jnp.clip(jax.random.uniform(splits[5], (VIRTUALS,), jnp.float32, 0.2, 3.0), 0.2, 3.0)
    vv_mask = plant((jax.random.randint(splits[6], (TILES, TILES), 0, 4) < 3).astype(jnp.int32), jax.random.fold_in(splits[6], 1), 0, 1)
    pair_domain = plant((jax.random.randint(splits[7], (OCC_OWNED, OCC_SLAB, TILES), 0, 4) < 3).astype(jnp.int32), jax.random.fold_in(splits[7], 1), 0, 1)
    return dict(amplitudes=amplitudes, vv_factors=vv_factors, ov_factors=ov_factors, occ_energy_i=occ_energy_i, occ_energy_j=occ_energy_j, virt_energy=virt_energy, vv_mask=vv_mask, pair_domain=pair_domain)


def reference(amplitudes, vv_factors, ov_factors, occ_energy_i, occ_energy_j, virt_energy, vv_mask, pair_domain):
    domain = jnp.repeat(pair_domain, TILE_SIZE, axis=2).astype(jnp.float32)
    pair_mask = domain[:, :, :, None] * domain[:, :, None, :]
    masked = (amplitudes.astype(jnp.float32) * pair_mask).astype(jnp.bfloat16)
    grid = jnp.repeat(jnp.repeat(vv_mask, TILE_SIZE, axis=0), TILE_SIZE, axis=1).astype(jnp.bfloat16)
    factors = vv_factors * grid[None]
    masked_wide = masked.astype(jnp.float32)

    def ladder_step(accum, factor):
        wide = factor.astype(jnp.float32)
        weighted = jnp.einsum('ac,ijcd->ijad', wide, masked_wide).astype(jnp.bfloat16)
        weighted = lax.optimization_barrier(weighted).astype(jnp.float32)
        return accum + jnp.einsum('ijad,bd->ijab', weighted, wide), None

    ladder, unused = lax.scan(ladder_step, jnp.zeros(masked.shape, jnp.float32), factors)
    mixed = (2.0 * masked_wide - jnp.swapaxes(masked_wide, 2, 3)).astype(jnp.bfloat16)
    ov_wide = ov_factors.astype(jnp.float32)
    zeta = jnp.einsum('ikac,qkc->iaq', mixed.astype(jnp.float32), ov_wide)
    cycle = jnp.einsum('iaq,qjb->ijab', zeta, ov_wide, precision=lax.Precision.HIGHEST)
    denom = (virt_energy[None, None, :, None] + virt_energy[None, None, None, :]
             - occ_energy_i[:, None, None, None] - occ_energy_j[None, :, None, None])
    return ((ladder + cycle) * pair_mask / denom).astype(jnp.bfloat16)
```

```python
import functools

import jax
import jax.numpy as jnp
from jax import lax
from jax.experimental import pallas as pl
from jax.experimental.pallas import tpu as pltpu
from jax.sharding import PartitionSpec as P

TILE_SIZE = 128
GROUP = 4
MESH = pl.DeviceIdType.MESH
F32 = jnp.float32
BF16 = jnp.bfloat16


def dot_nn(left, right):
    return lax.dot_general(left, right, (((1,), (0,)), ((), ())), preferred_element_type=F32)


def dot_nt(left, right):
    return lax.dot_general(left, right, (((1,), (1,)), ((), ())), preferred_element_type=F32)


def over_tiles(index, values):
    picked = jnp.zeros(index.shape, F32)
    for tile, value in enumerate(values):
        picked = jnp.where(index // TILE_SIZE == tile, value, picked)
    return picked


def kernel(
    columns,
    planes,
    amp_ref,
    ov_ref,
    occ_i_ref,
    occ_j_ref,
    energy_ref,
    vv_mask_ref,
    domain_ref,
    vv_ref,
    out_ref,
    factors,
    lines,
    pairs,
    ov_mine,
    zetas,
    terms,
    parts,
    load_sem,
    line_send,
    line_recv,
    pair_send,
    pair_recv,
    ov_send,
    ov_recv,
    zeta_send,
    zeta_recv,
    part_send,
    part_recv,
):
    pair = lax.axis_index("pair")
    virt = lax.axis_index("virt")
    integ = lax.axis_index("integ")
    share, wide = amp_ref.shape[2], amp_ref.shape[3]
    aux = vv_ref.shape[0]
    tiles = wide // TILE_SIZE
    held = planes // columns
    home = integ // held
    slot = integ % held

    def remote(src, dst, send_sem, recv_sem, to_virt, to_integ):
        return pltpu.make_async_remote_copy(
            src_ref=src,
            dst_ref=dst,
            send_sem=send_sem,
            recv_sem=recv_sem,
            device_id=(pair, to_virt, to_integ),
            device_id_type=MESH,
        )

    def rows(which):
        return pl.ds(pl.multiple_of(which * share, share), share)

    load = pltpu.make_async_copy(vv_ref, factors, load_sem)
    load.start()

    barrier = pltpu.get_barrier_semaphore()

    def greet(to_virt, to_integ):
        pl.semaphore_signal(
            barrier, inc=1, device_id=(pair, to_virt, to_integ), device_id_type=MESH
        )

    for step in range(1, planes):
        greet(virt, lax.rem(integ + step, planes))
    for step in range(1, columns):
        greet(lax.rem(virt + step, columns), integ)

    @pl.when(home != virt)
    def _():
        for step in range(1, planes):
            greet(home, lax.rem(integ + step, planes))

    domain = [domain_ref[0, 0, tile].astype(F32) for tile in range(tiles)]
    row_index = virt * share + lax.broadcasted_iota(jnp.int32, (share, wide), 0)
    col_index = lax.broadcasted_iota(jnp.int32, (share, wide), 1)
    pair_mask = over_tiles(row_index, domain) * over_tiles(col_index, domain)
    lines[integ] = (amp_ref[0, 0].astype(F32) * pair_mask).astype(BF16)

    own_home = jnp.where(home == virt, 1, 0)
    pl.semaphore_wait(barrier, planes - 1 + (columns - 1) * (held + 1 - own_home))

    def line_copy(step):
        return remote(
            lines.at[integ],
            lines.at[integ],
            line_send.at[step],
            line_recv.at[integ],
            virt,
            lax.rem(integ + step, planes),
        )

    def ov_copy(step):
        to_integ = lax.rem(integ + step, planes)
        return remote(
            ov_ref.at[pl.ds(pl.multiple_of(to_integ * aux, aux), aux)],
            ov_mine.at[slot],
            ov_send.at[step],
            ov_recv.at[slot],
            virt,
            to_integ,
        )

    def pair_copy(which):
        return remote(
            lines.at[which],
            pairs.at[which % held, rows(virt)],
            pair_send.at[which],
            pair_recv.at[(which % held) * columns + virt],
            which // held,
            integ,
        )

    def forward(which):
        @pl.when(which // held != virt)
        def _():
            pair_copy(which).start()

        @pl.when(which // held == virt)
        def _():
            pairs[which % held, rows(virt)] = lines[which]

    for step in range(1, planes):
        line_copy(step).start()
    forward(integ)

    @pl.when(home == virt)
    def _():
        for step in range(1, planes):
            ov_copy(step).start()
        ov_mine[slot] = ov_ref[pl.ds(pl.multiple_of(integ * aux, aux), aux)]

    row_in = lax.broadcasted_iota(jnp.int32, (wide, wide), 0) // TILE_SIZE
    col_in = lax.broadcasted_iota(jnp.int32, (wide, wide), 1) // TILE_SIZE
    grid = jnp.zeros((wide, wide), F32)
    for first in range(tiles):
        for second in range(tiles):
            here = jnp.logical_and(row_in == first, col_in == second)
            grid = jnp.where(here, vv_mask_ref[first, second].astype(F32), grid)
    grid = grid.astype(BF16)
    energy = jnp.broadcast_to(energy_ref[...], (share, wide))
    energy_rows = jnp.sum(jnp.where(col_index == row_index, energy, 0.0), axis=1, keepdims=True)
    denom = energy_rows + energy - occ_i_ref[0] - occ_j_ref[0]
    scale = pair_mask / denom
    load.wait()

    @pl.loop(0, aux)
    def _(q):
        factors[q] = factors[q] * grid

    for step in range(1, planes):
        which = lax.rem(integ + step, planes)
        line_copy_in = remote(
            lines.at[which], lines.at[which], line_send.at[step], line_recv.at[which], virt, which
        )
        line_copy_in.wait_recv()
        forward(which)

    for first in range(held):
        @pl.when(jnp.logical_or(home != virt, slot != first))
        def _(first=first):
            ov_in = remote(
                ov_mine.at[first], ov_mine.at[first], ov_send.at[0], ov_recv.at[first], virt, integ
            )
            ov_in.wait_recv()

        for step in range(1, columns):
            source = lax.rem(virt + step, columns)
            landed = pairs.at[first, rows(source)]
            remote(
                landed,
                landed,
                pair_send.at[0],
                pair_recv.at[first * columns + source],
                source,
                integ,
            ).wait_recv()

    zeta_part = jnp.zeros((aux, wide), F32)
    for first in range(held):
        amps = pairs[first]
        zeta_part += 2.0 * dot_nt(ov_mine[first], amps) - dot_nn(ov_mine[first], amps)
    zetas[virt] = zeta_part

    def zeta_copy(step):
        return remote(
            zetas.at[virt],
            zetas.at[virt],
            zeta_send.at[step],
            zeta_recv.at[virt],
            lax.rem(virt + step, columns),
            integ,
        )

    for step in range(1, columns):
        zeta_copy(step).start()

    def ladder(first):
        amps = pairs[first]

        def add(group, total):
            block = factors[pl.ds(group * GROUP, GROUP)]
            weighted = dot_nn(block.reshape(GROUP * wide, wide), amps).astype(BF16)
            for q in range(GROUP):
                total = total + dot_nt(weighted[q * wide:(q + 1) * wide], block[q])
            return total

        return lax.fori_loop(0, aux // GROUP, add, jnp.zeros((wide, wide), F32))

    def cycle(first, upper, lower):
        return dot_nn(upper, ov_mine[first]) + dot_nn(lower, ov_mine[first])

    def zeta_halves():
        for step in range(1, columns):
            source = lax.rem(virt + step, columns)
            landed = zetas.at[source]
            remote(
                landed, landed, zeta_send.at[0], zeta_recv.at[source], source, integ
            ).wait_recv()
        zeta = zetas[0]
        for column in range(1, columns):
            zeta = zeta + zetas[column]
        zeta = zeta.T
        upper = zeta.astype(BF16)
        return upper, (zeta - upper.astype(F32)).astype(BF16)

    def part_copy(first, row):
        return remote(
            terms.at[first, pl.ds(row * share, share)],
            parts.at[integ],
            part_send.at[first * columns + row],
            part_recv.at[integ],
            row,
            virt * held + first,
        )

    def hand_over(first):
        for row in range(columns):
            mine = jnp.logical_and(virt == row, virt * held + first == integ)

            @pl.when(jnp.logical_not(mine))
            def _(row=row):
                part_copy(first, row).start()

            @pl.when(mine)
            def _(row=row):
                parts[integ] = terms[first, pl.ds(row * share, share)]

    if held == 1:
        total = ladder(0)
        upper, lower = zeta_halves()
        terms[0] = (total + cycle(0, upper, lower)).astype(BF16)
        hand_over(0)
    else:
        upper, lower = zeta_halves()

        @pl.loop(0, held)
        def _(first):
            terms[first] = (ladder(first) + cycle(first, upper, lower)).astype(BF16)
            hand_over(first)

    for source in range(planes):
        @pl.when(jnp.logical_or(home != virt, integ != source))
        def _(source=source):
            remote(
                parts.at[source],
                parts.at[source],
                part_send.at[0],
                part_recv.at[source],
                home,
                integ,
            ).wait_recv()

    total = parts[0].astype(F32)
    for source in range(1, planes):
        total = total + parts[source].astype(F32)
    out_ref[0, 0] = (total * scale).astype(BF16)

    for step in range(1, planes):
        line_copy(step).wait_send()
    for step in range(1, columns):
        zeta_copy(step).wait_send()
    for which in range(planes):
        @pl.when(which // held != virt)
        def _(which=which):
            pair_copy(which).wait_send()

    @pl.when(home == virt)
    def _():
        for step in range(1, planes):
            ov_copy(step).wait_send()

    for first in range(held):
        for row in range(columns):
            mine = jnp.logical_and(virt == row, virt * held + first == integ)

            @pl.when(jnp.logical_not(mine))
            def _(first=first, row=row):
                part_copy(first, row).wait_send()


def body(
    columns,
    planes,
    amplitudes,
    vv_factors,
    ov_factors,
    occ_energy_i,
    occ_energy_j,
    virt_energy,
    vv_mask,
    pair_domain,
):
    share, wide = amplitudes.shape[2:]
    aux = vv_factors.shape[0]
    held = planes // columns
    vmem = pl.BlockSpec(memory_space=pltpu.VMEM)
    smem = pl.BlockSpec(memory_space=pltpu.SMEM)
    dma = pltpu.SemaphoreType.DMA
    return pl.pallas_call(
        functools.partial(kernel, columns, planes),
        out_shape=jax.ShapeDtypeStruct(amplitudes.shape, BF16),
        in_specs=[vmem, vmem, smem, smem, vmem, smem, smem, pl.BlockSpec(memory_space=pl.ANY)],
        out_specs=vmem,
        scratch_shapes=[
            pltpu.VMEM((aux, wide, wide), BF16),
            pltpu.VMEM((planes, share, wide), BF16),
            pltpu.VMEM((held, wide, wide), BF16),
            pltpu.VMEM((held, aux, wide), BF16),
            pltpu.VMEM((columns, aux, wide), F32),
            pltpu.VMEM((held, wide, wide), BF16),
            pltpu.VMEM((planes, share, wide), BF16),
            dma,
            dma((planes,)),
            dma((planes,)),
            dma((planes,)),
            dma((planes,)),
            dma((planes,)),
            dma((held,)),
            dma((columns,)),
            dma((columns,)),
            dma((planes,)),
            dma((planes,)),
        ],
        compiler_params=pltpu.CompilerParams(
            collective_id=0, has_side_effects=True, vmem_limit_bytes=40 * 1024 * 1024
        ),
        cost_estimate=pl.CostEstimate(
            flops=4 * held * aux * wide**3, bytes_accessed=2 * aux * wide * wide, transcendentals=0
        ),
    )(
        amplitudes,
        ov_factors.reshape(ov_factors.shape[0], wide),
        occ_energy_i,
        occ_energy_j,
        virt_energy.reshape(1, wide),
        vv_mask,
        pair_domain,
        vv_factors,
    )


def solution(mesh):
    placed = (
        P("pair", "integ", "virt", None),
        P("integ", None, None),
        P(None, "integ", None),
        P("pair"),
        P("integ"),
        P(),
        P(),
        P("pair", "integ", None),
    )
    return jax.shard_map(
        functools.partial(body, mesh.shape["virt"], mesh.shape["integ"]),
        mesh=mesh,
        in_specs=placed,
        out_specs=P("pair", "integ", "virt", None),
        check_vma=False,
    )
```

```python
import functools

import jax
import jax.numpy as jnp
from jax import lax
from jax.experimental import pallas as pl
from jax.experimental.pallas import tpu as pltpu
from jax.sharding import PartitionSpec as P

TILE_SIZE = 128
GROUP = 4
MESH = pl.DeviceIdType.MESH
F32 = jnp.float32
BF16 = jnp.bfloat16


def dot_nn(left, right):
    return lax.dot_general(left, right, (((1,), (0,)), ((), ())), preferred_element_type=F32)


def dot_nt(left, right):
    return lax.dot_general(left, right, (((1,), (1,)), ((), ())), preferred_element_type=F32)


def over_tiles(index, values):
    picked = jnp.zeros(index.shape, F32)
    for tile, value in enumerate(values):
        picked = jnp.where(index // TILE_SIZE == tile, value, picked)
    return picked


def kernel(
    columns,
    planes,
    amp_hbm,
    ov_hbm,
    occ_i_hbm,
    occ_j_hbm,
    energy_hbm,
    vv_mask_hbm,
    domain_hbm,
    vv_hbm,
    out_ref,
    amp_ref,
    ov_ref,
    occ_i_ref,
    occ_j_ref,
    energy_ref,
    vv_mask_ref,
    domain_ref,
    factors,
    lines,
    pairs,
    ov_mine,
    zetas,
    terms,
    hops,
    parts,
    load_sem,
    line_send,
    line_recv,
    pair_send,
    pair_recv,
    ov_send,
    ov_recv,
    zeta_send,
    zeta_recv,
    hop_send,
    hop_recv,
    part_send,
    part_recv,
):
    pair = lax.axis_index("pair")
    virt = lax.axis_index("virt")
    integ = lax.axis_index("integ")
    share, wide = amp_ref.shape[2], amp_ref.shape[3]
    aux = factors.shape[0]
    tiles = wide // TILE_SIZE
    held = planes // columns
    home = integ // held
    slot = integ % held

    def remote(src, dst, send_sem, recv_sem, to_virt, to_integ):
        return pltpu.make_async_remote_copy(
            src_ref=src,
            dst_ref=dst,
            send_sem=send_sem,
            recv_sem=recv_sem,
            device_id=(pair, to_virt, to_integ),
            device_id_type=MESH,
        )

    def rows(which):
        return pl.ds(pl.multiple_of(which * share, share), share)

    loads = [
        pltpu.make_async_copy(src, dst, load_sem.at[which])
        for which, (src, dst) in enumerate(
            (
                (amp_hbm, amp_ref),
                (domain_hbm, domain_ref),
                (ov_hbm, ov_ref),
                (vv_mask_hbm, vv_mask_ref),
                (energy_hbm, energy_ref),
                (occ_i_hbm, occ_i_ref),
                (occ_j_hbm, occ_j_ref),
                (vv_hbm, factors),
            )
        )
    ]
    for load in loads:
        load.start()

    barrier = pltpu.get_barrier_semaphore()

    def greet(to_virt, to_integ):
        pl.semaphore_signal(
            barrier, inc=1, device_id=(pair, to_virt, to_integ), device_id_type=MESH
        )

    for step in range(1, planes):
        greet(virt, lax.rem(integ + step, planes))
    for step in range(1, columns):
        greet(lax.rem(virt + step, columns), integ)

    loads[0].wait()
    loads[1].wait()

    domain = [domain_ref[0, 0, tile].astype(F32) for tile in range(tiles)]
    row_index = virt * share + lax.broadcasted_iota(jnp.int32, (share, wide), 0)
    col_index = lax.broadcasted_iota(jnp.int32, (share, wide), 1)
    pair_mask = over_tiles(row_index, domain) * over_tiles(col_index, domain)
    lines[integ] = (amp_ref[0, 0].astype(F32) * pair_mask).astype(BF16)

    pl.semaphore_wait(barrier, planes + columns - 2)

    def line_copy(step):
        return remote(
            lines.at[integ],
            lines.at[integ],
            line_send.at[step],
            line_recv.at[integ],
            virt,
            lax.rem(integ + step, planes),
        )

    def ov_copy(step):
        to_integ = lax.rem(integ + step, planes)
        return remote(
            ov_ref.at[pl.ds(pl.multiple_of(to_integ * aux, aux), aux)],
            ov_mine.at[slot],
            ov_send.at[step],
            ov_recv.at[slot],
            virt,
            to_integ,
        )

    def pair_copy(which):
        return remote(
            lines.at[which],
            pairs.at[which % held, rows(virt)],
            pair_send.at[which],
            pair_recv.at[(which % held) * columns + virt],
            which // held,
            integ,
        )

    def forward(which):
        @pl.when(which // held != virt)
        def _():
            pair_copy(which).start()

        @pl.when(which // held == virt)
        def _():
            pairs[which % held, rows(virt)] = lines[which]

    for step in range(1, planes):
        line_copy(step).start()
    forward(integ)
    loads[2].wait()

    @pl.when(home == virt)
    def _():
        for step in range(1, planes):
            ov_copy(step).start()
        ov_mine[slot] = ov_ref[pl.ds(pl.multiple_of(integ * aux, aux), aux)]

    for load in loads[3:7]:
        load.wait()

    row_in = lax.broadcasted_iota(jnp.int32, (wide, wide), 0) // TILE_SIZE
    col_in = lax.broadcasted_iota(jnp.int32, (wide, wide), 1) // TILE_SIZE
    grid = jnp.zeros((wide, wide), F32)
    for first in range(tiles):
        for second in range(tiles):
            here = jnp.logical_and(row_in == first, col_in == second)
            grid = jnp.where(here, vv_mask_ref[first, second].astype(F32), grid)
    grid = grid.astype(BF16)
    energy = jnp.broadcast_to(energy_ref[...], (share, wide))
    energy_rows = jnp.sum(jnp.where(col_index == row_index, energy, 0.0), axis=1, keepdims=True)
    denom = energy_rows + energy - occ_i_ref[0] - occ_j_ref[0]
    scale = pair_mask / denom
    loads[7].wait()

    @pl.loop(0, aux)
    def _(q):
        factors[q] = factors[q] * grid

    for step in range(1, planes):
        which = lax.rem(integ + step, planes)
        line_copy_in = remote(
            lines.at[which], lines.at[which], line_send.at[step], line_recv.at[which], virt, which
        )
        line_copy_in.wait_recv()
        forward(which)

    for first in range(held):
        @pl.when(jnp.logical_or(home != virt, slot != first))
        def _(first=first):
            ov_in = remote(
                ov_mine.at[first], ov_mine.at[first], ov_send.at[0], ov_recv.at[first], virt, integ
            )
            ov_in.wait_recv()

        for step in range(1, columns):
            source = lax.rem(virt + step, columns)
            landed = pairs.at[first, rows(source)]
            remote(
                landed,
                landed,
                pair_send.at[0],
                pair_recv.at[first * columns + source],
                source,
                integ,
            ).wait_recv()

    zeta_part = jnp.zeros((aux, wide), F32)
    for first in range(held):
        amps = pairs[first]
        zeta_part += 2.0 * dot_nt(ov_mine[first], amps) - dot_nn(ov_mine[first], amps)
    zetas[virt] = zeta_part

    def zeta_copy(step):
        return remote(
            zetas.at[virt],
            zetas.at[virt],
            zeta_send.at[step],
            zeta_recv.at[virt],
            lax.rem(virt + step, columns),
            integ,
        )

    for step in range(1, columns):
        zeta_copy(step).start()

    def ladder(first):
        amps = pairs[first]

        def add(group, total):
            block = factors[pl.ds(group * GROUP, GROUP)]
            weighted = dot_nn(block.reshape(GROUP * wide, wide), amps).astype(BF16)
            for q in range(GROUP):
                total = total + dot_nt(weighted[q * wide:(q + 1) * wide], block[q])
            return total

        return lax.fori_loop(0, aux // GROUP, add, jnp.zeros((wide, wide), F32))

    def cycle(first, upper, lower):
        return dot_nn(upper, ov_mine[first]) + dot_nn(lower, ov_mine[first])

    def zeta_halves():
        for step in range(1, columns):
            source = lax.rem(virt + step, columns)
            landed = zetas.at[source]
            remote(
                landed, landed, zeta_send.at[0], zeta_recv.at[source], source, integ
            ).wait_recv()
        zeta = zetas[0]
        for column in range(1, columns):
            zeta = zeta + zetas[column]
        zeta = zeta.T
        upper = zeta.astype(BF16)
        return upper, (zeta - upper.astype(F32)).astype(BF16)

    def hop_copy(first, step):
        row = lax.rem(virt + step, columns)
        return remote(
            terms.at[first, rows(row)],
            hops.at[virt * held + first],
            hop_send.at[first * columns + step],
            hop_recv.at[virt * held + first],
            row,
            integ,
        )

    def part_copy(which):
        return remote(
            hops.at[which],
            parts.at[integ],
            part_send.at[which],
            part_recv.at[integ],
            virt,
            which,
        )

    def pass_on(which):
        @pl.when(which != integ)
        def _():
            part_copy(which).start()

        @pl.when(which == integ)
        def _():
            parts[integ] = hops[which]

    def hand_over(first):
        for step in range(1, columns):
            hop_copy(first, step).start()
        which = virt * held + first
        hops[which] = terms[first, rows(virt)]
        pass_on(which)

    if held == 1:
        total = ladder(0)
        upper, lower = zeta_halves()
        terms[0] = (total + cycle(0, upper, lower)).astype(BF16)
        hand_over(0)
    else:
        upper, lower = zeta_halves()

        @pl.loop(0, held)
        def _(first):
            terms[first] = (ladder(first) + cycle(first, upper, lower)).astype(BF16)
            hand_over(first)

    for step in range(1, columns):
        source = lax.rem(virt + step, columns)
        for first in range(held):
            which = source * held + first
            landed = hops.at[which]
            remote(
                landed, landed, hop_send.at[0], hop_recv.at[which], source, integ
            ).wait_recv()
            pass_on(which)

    for step in range(1, planes):
        source = lax.rem(integ + step, planes)
        landed = parts.at[source]
        remote(
            landed, landed, part_send.at[0], part_recv.at[source], virt, source
        ).wait_recv()

    total = parts[0].astype(F32)
    for source in range(1, planes):
        total = total + parts[source].astype(F32)
    out_ref[0, 0] = (total * scale).astype(BF16)

    for step in range(1, planes):
        line_copy(step).wait_send()
    for step in range(1, columns):
        zeta_copy(step).wait_send()
    for which in range(planes):
        @pl.when(which // held != virt)
        def _(which=which):
            pair_copy(which).wait_send()

    @pl.when(home == virt)
    def _():
        for step in range(1, planes):
            ov_copy(step).wait_send()

    for first in range(held):
        for step in range(1, columns):
            hop_copy(first, step).wait_send()
    for step in range(1, planes):
        part_copy(lax.rem(integ + step, planes)).wait_send()


def body(
    columns,
    planes,
    amplitudes,
    vv_factors,
    ov_factors,
    occ_energy_i,
    occ_energy_j,
    virt_energy,
    vv_mask,
    pair_domain,
):
    share, wide = amplitudes.shape[2:]
    aux = vv_factors.shape[0]
    held = planes // columns
    vmem = pl.BlockSpec(memory_space=pltpu.VMEM)
    smem = pltpu.SMEM
    dma = pltpu.SemaphoreType.DMA
    return pl.pallas_call(
        functools.partial(kernel, columns, planes),
        out_shape=jax.ShapeDtypeStruct(amplitudes.shape, BF16),
        in_specs=[pl.BlockSpec(memory_space=pltpu.HBM)] * 8,
        out_specs=vmem,
        scratch_shapes=[
            pltpu.VMEM(amplitudes.shape, BF16),
            pltpu.VMEM((ov_factors.shape[0], wide), BF16),
            smem(occ_energy_i.shape, F32),
            smem(occ_energy_j.shape, F32),
            pltpu.VMEM((1, wide), F32),
            smem(vv_mask.shape, jnp.int32),
            smem(pair_domain.shape, jnp.int32),
            pltpu.VMEM((aux, wide, wide), BF16),
            pltpu.VMEM((planes, share, wide), BF16),
            pltpu.VMEM((held, wide, wide), BF16),
            pltpu.VMEM((held, aux, wide), BF16),
            pltpu.VMEM((columns, aux, wide), F32),
            pltpu.VMEM((held, wide, wide), BF16),
            pltpu.VMEM((planes, share, wide), BF16),
            pltpu.VMEM((planes, share, wide), BF16),
            dma((8,)),
            dma((planes,)),
            dma((planes,)),
            dma((planes,)),
            dma((planes,)),
            dma((planes,)),
            dma((held,)),
            dma((columns,)),
            dma((columns,)),
            dma((planes,)),
            dma((planes,)),
            dma((planes,)),
            dma((planes,)),
        ],
        compiler_params=pltpu.CompilerParams(
            collective_id=0, has_side_effects=True, vmem_limit_bytes=60 * 1024 * 1024
        ),
        cost_estimate=pl.CostEstimate(
            flops=4 * held * aux * wide**3, bytes_accessed=2 * aux * wide * wide, transcendentals=0
        ),
    )(
        amplitudes,
        ov_factors.reshape(ov_factors.shape[0], wide),
        occ_energy_i,
        occ_energy_j,
        virt_energy.reshape(1, wide),
        vv_mask,
        pair_domain,
        vv_factors,
    )


def solution(mesh):
    placed = (
        P("pair", "integ", "virt", None),
        P("integ", None, None),
        P(None, "integ", None),
        P("pair"),
        P("integ"),
        P(),
        P(),
        P("pair", "integ", None),
    )
    return jax.shard_map(
        functools.partial(body, mesh.shape["virt"], mesh.shape["integ"]),
        mesh=mesh,
        in_specs=placed,
        out_specs=P("pair", "integ", "virt", None),
        check_vma=False,
    )
```

```python
import functools

import jax
import jax.numpy as jnp
from jax import lax
from jax.experimental import pallas as pl
from jax.experimental.pallas import tpu as pltpu
from jax.sharding import PartitionSpec as P

TILE_SIZE = 128
GROUP = 8
HALVES = 2
MESH = pl.DeviceIdType.MESH
F32 = jnp.float32
BF16 = jnp.bfloat16


def dot_nn(left, right):
    return lax.dot_general(left, right, (((1,), (0,)), ((), ())), preferred_element_type=F32)


def dot_nt(left, right):
    return lax.dot_general(left, right, (((1,), (1,)), ((), ())), preferred_element_type=F32)


def over_tiles(index, values):
    picked = jnp.zeros(index.shape, F32)
    for tile, value in enumerate(values):
        picked = jnp.where(index // TILE_SIZE == tile, value, picked)
    return picked


def kernel(
    columns,
    planes,
    amp_hbm,
    ov_hbm,
    occ_i_hbm,
    occ_j_hbm,
    energy_hbm,
    vv_mask_hbm,
    domain_hbm,
    vv_hbm,
    out_ref,
    amp_ref,
    ov_ref,
    occ_i_ref,
    occ_j_ref,
    energy_ref,
    vv_mask_ref,
    domain_ref,
    factors,
    line,
    pairs,
    ov_mine,
    zetas,
    zeta_rows,
    terms,
    hops,
    parts,
    load_sem,
    pair_send,
    pair_recv,
    ov_send,
    ov_recv,
    zeta_send,
    zeta_recv,
    hop_send,
    hop_recv,
    part_send,
    part_recv,
):
    pair = lax.axis_index("pair")
    virt = lax.axis_index("virt")
    integ = lax.axis_index("integ")
    share, wide = amp_ref.shape[2], amp_ref.shape[3]
    aux = factors.shape[0]
    tiles = wide // TILE_SIZE
    held = planes // columns
    home = integ // held
    slot = integ % held

    def remote(src, dst, send_sem, recv_sem, to_virt, to_integ):
        return pltpu.make_async_remote_copy(
            src_ref=src,
            dst_ref=dst,
            send_sem=send_sem,
            recv_sem=recv_sem,
            device_id=(pair, to_virt, to_integ),
            device_id_type=MESH,
        )

    def rows(which):
        return pl.ds(pl.multiple_of(which * share, share), share)

    loads = [
        pltpu.make_async_copy(src, dst, load_sem.at[which])
        for which, (src, dst) in enumerate(
            (
                (amp_hbm, amp_ref),
                (domain_hbm, domain_ref),
                (ov_hbm, ov_ref),
                (vv_mask_hbm, vv_mask_ref),
                (energy_hbm, energy_ref),
                (occ_i_hbm, occ_i_ref),
                (occ_j_hbm, occ_j_ref),
                (vv_hbm, factors),
            )
        )
    ]
    for load in loads:
        load.start()

    barrier = pltpu.get_barrier_semaphore()

    def greet(to_virt, to_integ):
        pl.semaphore_signal(
            barrier, inc=1, device_id=(pair, to_virt, to_integ), device_id_type=MESH
        )

    for step in range(1, planes):
        greet(virt, lax.rem(integ + step, planes))
    for step in range(1, columns):
        greet(lax.rem(virt + step, columns), integ)
    for first in range(held):
        @pl.when(virt * held + first != integ)
        def _(first=first):
            for step in range(1, columns):
                greet(lax.rem(virt + step, columns), virt * held + first)

    loads[0].wait()
    loads[1].wait()

    domain = [domain_ref[0, 0, tile].astype(F32) for tile in range(tiles)]
    row_index = virt * share + lax.broadcasted_iota(jnp.int32, (share, wide), 0)
    col_index = lax.broadcasted_iota(jnp.int32, (share, wide), 1)
    pair_mask = over_tiles(row_index, domain) * over_tiles(col_index, domain)
    line[...] = (amp_ref[0, 0].astype(F32) * pair_mask).astype(BF16)

    away = jnp.where(home != virt, planes - 1, 0)
    pl.semaphore_wait(barrier, planes + columns - 2 + away)

    def ov_copy(step):
        to_integ = lax.rem(integ + step, planes)
        return remote(
            ov_ref.at[pl.ds(pl.multiple_of(to_integ * aux, aux), aux)],
            ov_mine.at[slot],
            ov_send.at[step],
            ov_recv.at[slot],
            virt,
            to_integ,
        )

    def pair_copy(to_integ):
        return remote(
            line,
            pairs.at[slot, rows(virt)],
            pair_send.at[to_integ],
            pair_recv.at[slot * columns + virt],
            home,
            to_integ,
        )

    for turn in range(planes):
        to_integ = jnp.where(2 * integ < planes, planes - 1 - turn, turn)

        @pl.when(jnp.logical_or(home != virt, to_integ != integ))
        def _(to_integ=to_integ):
            pair_copy(to_integ).start()

    @pl.when(home == virt)
    def _():
        pairs[slot, rows(virt)] = line[...]

    loads[2].wait()

    @pl.when(home == virt)
    def _():
        for step in range(1, planes):
            ov_copy(step).start()
        ov_mine[slot] = ov_ref[pl.ds(pl.multiple_of(integ * aux, aux), aux)]

    for load in loads[3:7]:
        load.wait()

    row_in = lax.broadcasted_iota(jnp.int32, (wide, wide), 0) // TILE_SIZE
    col_in = lax.broadcasted_iota(jnp.int32, (wide, wide), 1) // TILE_SIZE
    grid = jnp.zeros((wide, wide), F32)
    for first in range(tiles):
        for second in range(tiles):
            here = jnp.logical_and(row_in == first, col_in == second)
            grid = jnp.where(here, vv_mask_ref[first, second].astype(F32), grid)
    grid = grid.astype(BF16)
    energy = jnp.broadcast_to(energy_ref[...], (share, wide))
    energy_rows = jnp.sum(jnp.where(col_index == row_index, energy, 0.0), axis=1, keepdims=True)
    denom = energy_rows + energy - occ_i_ref[0] - occ_j_ref[0]
    scale = pair_mask / denom
    loads[7].wait()

    @pl.loop(0, aux)
    def _(q):
        factors[q] = factors[q] * grid

    for first in range(held):
        @pl.when(virt * held + first != integ)
        def _(first=first):
            ov_in = remote(
                ov_mine.at[first], ov_mine.at[first], ov_send.at[0], ov_recv.at[first], virt, integ
            )
            ov_in.wait_recv()

        for source in range(columns):
            @pl.when(jnp.logical_or(virt * held + first != integ, source != virt))
            def _(first=first, source=source):
                landed = pairs.at[first, rows(source)]
                remote(
                    landed,
                    landed,
                    pair_send.at[0],
                    pair_recv.at[first * columns + source],
                    virt,
                    integ,
                ).wait_recv()

    zeta_part = jnp.zeros((aux, wide), F32)
    for first in range(held):
        amps = pairs[first]
        zeta_part += 2.0 * dot_nt(ov_mine[first], amps) - dot_nn(ov_mine[first], amps)
    zetas[virt] = zeta_part

    def zeta_copy(step):
        return remote(
            zetas.at[virt],
            zetas.at[virt],
            zeta_send.at[step],
            zeta_recv.at[virt],
            lax.rem(virt + step, columns),
            integ,
        )

    for step in range(1, columns):
        zeta_copy(step).start()

    depth = wide // HALVES
    near = columns // HALVES
    my_half = virt // near

    def lines_of(half):
        return pl.ds(pl.multiple_of(half * depth, depth), depth)

    def ladder(first, half):
        amps = pairs[first]

        def add(group, total):
            block = factors[pl.ds(group * GROUP, GROUP)]
            some = factors[pl.ds(group * GROUP, GROUP), lines_of(half)]
            weighted = dot_nn(some.reshape(GROUP * depth, wide), amps).astype(BF16)
            for q in range(GROUP):
                total = total + dot_nt(weighted[q * depth:(q + 1) * depth], block[q])
            return total

        return lax.fori_loop(0, aux // GROUP, add, jnp.zeros((depth, wide), F32))

    def cycle(first, half):
        upper, lower = zeta_rows[0, lines_of(half)], zeta_rows[1, lines_of(half)]
        return dot_nn(upper, ov_mine[first]) + dot_nn(lower, ov_mine[first])

    def gather_zeta():
        for step in range(1, columns):
            source = lax.rem(virt + step, columns)
            landed = zetas.at[source]
            remote(
                landed, landed, zeta_send.at[0], zeta_recv.at[source], source, integ
            ).wait_recv()
        zeta = zetas[0]
        for column in range(1, columns):
            zeta = zeta + zetas[column]
        zeta = zeta.T
        upper = zeta.astype(BF16)
        zeta_rows[0] = upper
        zeta_rows[1] = (zeta - upper.astype(F32)).astype(BF16)

    def hop_copy(first, row):
        return remote(
            terms.at[first, rows(row)],
            hops.at[virt * held + first],
            hop_send.at[first * columns + row],
            hop_recv.at[virt * held + first],
            row,
            integ,
        )

    def part_copy(which):
        return remote(
            hops.at[which],
            parts.at[integ],
            part_send.at[which],
            part_recv.at[integ],
            virt,
            which,
        )

    def pass_on(which):
        @pl.when(which != integ)
        def _():
            part_copy(which).start()

        @pl.when(which == integ)
        def _():
            parts[integ] = hops[which]

    def hand_over(first, half):
        for step in range(near):
            row = half * near + lax.rem(virt + 1 + step, near)

            @pl.when(row != virt)
            def _(row=row):
                hop_copy(first, row).start()

            @pl.when(row == virt)
            def _(row=row):
                hops[virt * held + first] = terms[first, rows(row)]
                pass_on(virt * held + first)

    def work(first):
        for turn in range(HALVES):
            half = lax.rem(my_half + 1 + turn, HALVES)
            total = ladder(first, half)
            if held == 1 and turn == 0:
                gather_zeta()
            terms[first, lines_of(half)] = (total + cycle(first, half)).astype(BF16)
            hand_over(first, half)

    if held == 1:
        work(0)
    else:
        gather_zeta()
        pl.loop(0, held)(work)

    for turn in range(HALVES):
        half = lax.rem(my_half + 1 + turn, HALVES)
        for step in range(near):
            source = half * near + lax.rem(virt + 1 + step, near)

            @pl.when(source != virt)
            def _(source=source):
                for first in range(held):
                    which = source * held + first
                    landed = hops.at[which]
                    remote(
                        landed, landed, hop_send.at[0], hop_recv.at[which], source, integ
                    ).wait_recv()
                    pass_on(which)

    for step in range(1, planes):
        source = lax.rem(integ + step, planes)
        landed = parts.at[source]
        remote(
            landed, landed, part_send.at[0], part_recv.at[source], virt, source
        ).wait_recv()

    total = parts[0].astype(F32)
    for source in range(1, planes):
        total = total + parts[source].astype(F32)
    out_ref[0, 0] = (total * scale).astype(BF16)

    for step in range(1, columns):
        zeta_copy(step).wait_send()
    for to_integ in range(planes):
        @pl.when(jnp.logical_or(home != virt, to_integ != integ))
        def _(to_integ=to_integ):
            pair_copy(to_integ).wait_send()

    @pl.when(home == virt)
    def _():
        for step in range(1, planes):
            ov_copy(step).wait_send()

    for first in range(held):
        for step in range(1, columns):
            hop_copy(first, lax.rem(virt + step, columns)).wait_send()
    for step in range(1, planes):
        part_copy(lax.rem(integ + step, planes)).wait_send()


def body(
    columns,
    planes,
    amplitudes,
    vv_factors,
    ov_factors,
    occ_energy_i,
    occ_energy_j,
    virt_energy,
    vv_mask,
    pair_domain,
):
    share, wide = amplitudes.shape[2:]
    aux = vv_factors.shape[0]
    held = planes // columns
    vmem = pl.BlockSpec(memory_space=pltpu.VMEM)
    smem = pltpu.SMEM
    dma = pltpu.SemaphoreType.DMA
    return pl.pallas_call(
        functools.partial(kernel, columns, planes),
        out_shape=jax.ShapeDtypeStruct(amplitudes.shape, BF16),
        in_specs=[pl.BlockSpec(memory_space=pltpu.HBM)] * 8,
        out_specs=vmem,
        scratch_shapes=[
            pltpu.VMEM(amplitudes.shape, BF16),
            pltpu.VMEM((ov_factors.shape[0], wide), BF16),
            smem(occ_energy_i.shape, F32),
            smem(occ_energy_j.shape, F32),
            pltpu.VMEM((1, wide), F32),
            smem(vv_mask.shape, jnp.int32),
            smem(pair_domain.shape, jnp.int32),
            pltpu.VMEM((aux, wide, wide), BF16),
            pltpu.VMEM((share, wide), BF16),
            pltpu.VMEM((held, wide, wide), BF16),
            pltpu.VMEM((held, aux, wide), BF16),
            pltpu.VMEM((columns, aux, wide), F32),
            pltpu.VMEM((2, wide, aux), BF16),
            pltpu.VMEM((held, wide, wide), BF16),
            pltpu.VMEM((planes, share, wide), BF16),
            pltpu.VMEM((planes, share, wide), BF16),
            dma((8,)),
            dma((planes,)),
            dma((planes,)),
            dma((planes,)),
            dma((held,)),
            dma((columns,)),
            dma((columns,)),
            dma((planes,)),
            dma((planes,)),
            dma((planes,)),
            dma((planes,)),
        ],
        compiler_params=pltpu.CompilerParams(
            collective_id=0, has_side_effects=True, vmem_limit_bytes=60 * 1024 * 1024
        ),
        cost_estimate=pl.CostEstimate(
            flops=4 * held * aux * wide**3, bytes_accessed=2 * aux * wide * wide, transcendentals=0
        ),
    )(
        amplitudes,
        ov_factors.reshape(ov_factors.shape[0], wide),
        occ_energy_i,
        occ_energy_j,
        virt_energy.reshape(1, wide),
        vv_mask,
        pair_domain,
        vv_factors,
    )


def solution(mesh):
    placed = (
        P("pair", "integ", "virt", None),
        P("integ", None, None),
        P(None, "integ", None),
        P("pair"),
        P("integ"),
        P(),
        P(),
        P("pair", "integ", None),
    )
    return jax.shard_map(
        functools.partial(body, mesh.shape["virt"], mesh.shape["integ"]),
        mesh=mesh,
        in_specs=placed,
        out_specs=P("pair", "integ", "virt", None),
        check_vma=False,
    )
```

```python
import functools

import jax
import jax.numpy as jnp
from jax import lax
from jax.experimental import pallas as pl
from jax.experimental.pallas import tpu as pltpu
from jax.sharding import PartitionSpec as P

TILE_SIZE = 128
GROUP = 8
HALVES = 2
MESH = pl.DeviceIdType.MESH
F32 = jnp.float32
BF16 = jnp.bfloat16


def dot_nn(left, right):
    return lax.dot_general(left, right, (((1,), (0,)), ((), ())), preferred_element_type=F32)


def dot_nt(left, right):
    return lax.dot_general(left, right, (((1,), (1,)), ((), ())), preferred_element_type=F32)


def over_tiles(index, values):
    picked = jnp.zeros(index.shape, F32)
    for tile, value in enumerate(values):
        picked = jnp.where(index // TILE_SIZE == tile, value, picked)
    return picked


def kernel(
    columns,
    planes,
    amp_hbm,
    ov_hbm,
    occ_i_hbm,
    occ_j_hbm,
    energy_hbm,
    vv_mask_hbm,
    domain_hbm,
    vv_hbm,
    out_ref,
    ov_ref,
    occ_i_ref,
    occ_j_ref,
    energy_ref,
    vv_mask_ref,
    domain_ref,
    factors,
    domains,
    pairs,
    ov_mine,
    zetas,
    zeta_rows,
    terms,
    hops,
    parts,
    load_sem,
    pair_send,
    pair_recv,
    ov_send,
    ov_recv,
    domain_send,
    domain_recv,
    zeta_send,
    zeta_recv,
    hop_send,
    hop_recv,
    part_send,
    part_recv,
):
    pair = lax.axis_index("pair")
    virt = lax.axis_index("virt")
    integ = lax.axis_index("integ")
    share, wide = amp_hbm.shape[2], amp_hbm.shape[3]
    aux = factors.shape[0]
    tiles = wide // TILE_SIZE
    held = planes // columns
    home = integ // held
    slot = integ % held

    def remote(src, dst, send_sem, recv_sem, to_virt, to_integ):
        return pltpu.make_async_remote_copy(
            src_ref=src,
            dst_ref=dst,
            send_sem=send_sem,
            recv_sem=recv_sem,
            device_id=(pair, to_virt, to_integ),
            device_id_type=MESH,
        )

    def rows(which):
        return pl.ds(pl.multiple_of(which * share, share), share)

    loads = [
        pltpu.make_async_copy(src, dst, load_sem.at[which])
        for which, (src, dst) in enumerate(
            (
                (amp_hbm.at[0, 0], pairs.at[slot, rows(virt)]),
                (domain_hbm, domain_ref),
                (ov_hbm, ov_ref),
                (vv_mask_hbm, vv_mask_ref),
                (energy_hbm, energy_ref),
                (occ_i_hbm, occ_i_ref),
                (occ_j_hbm, occ_j_ref),
                (vv_hbm, factors),
            )
        )
    ]
    for load in loads[1:]:
        load.start()

    @pl.when(home == virt)
    def _():
        loads[0].start()

    barrier = pltpu.get_barrier_semaphore()

    def greet(to_virt, to_integ):
        pl.semaphore_signal(
            barrier, inc=1, device_id=(pair, to_virt, to_integ), device_id_type=MESH
        )

    for step in range(1, planes):
        greet(virt, lax.rem(integ + step, planes))
    for step in range(1, columns):
        greet(lax.rem(virt + step, columns), integ)
    for first in range(held):
        @pl.when(virt * held + first != integ)
        def _(first=first):
            for step in range(1, columns):
                greet(lax.rem(virt + step, columns), virt * held + first)

    away = jnp.where(home != virt, planes - 1, 0)
    pl.semaphore_wait(barrier, planes + columns - 2 + away)

    def ov_copy(step):
        to_integ = lax.rem(integ + step, planes)
        return remote(
            ov_ref.at[pl.ds(pl.multiple_of(to_integ * aux, aux), aux)],
            ov_mine.at[slot],
            ov_send.at[step],
            ov_recv.at[slot],
            virt,
            to_integ,
        )

    def pair_copy(to_integ):
        return remote(
            amp_hbm.at[0, 0],
            pairs.at[slot, rows(virt)],
            pair_send.at[to_integ],
            pair_recv.at[slot * columns + virt],
            home,
            to_integ,
        )

    for turn in range(planes):
        to_integ = jnp.where(2 * integ < planes, planes - 1 - turn, turn)

        @pl.when(jnp.logical_or(home != virt, to_integ != integ))
        def _(to_integ=to_integ):
            pair_copy(to_integ).start()

    loads[1].wait()
    domain = [domain_ref[0, 0, tile].astype(F32) for tile in range(tiles)]
    loads[2].wait()

    def domain_copy(step):
        return remote(
            domains.at[slot],
            domains.at[slot],
            domain_send.at[step],
            domain_recv.at[slot],
            virt,
            lax.rem(integ + step, planes),
        )

    @pl.when(home == virt)
    def _():
        for tile in range(tiles):
            domains[slot, :, pl.ds(tile * TILE_SIZE, TILE_SIZE)] = jnp.full(
                (domains.shape[1], TILE_SIZE), domain[tile], F32
            )
        for step in range(1, planes):
            domain_copy(step).start()
            ov_copy(step).start()
        ov_mine[slot] = ov_ref[pl.ds(pl.multiple_of(integ * aux, aux), aux)]

    for load in loads[3:7]:
        load.wait()

    row_in = lax.broadcasted_iota(jnp.int32, (wide, wide), 0) // TILE_SIZE
    col_in = lax.broadcasted_iota(jnp.int32, (wide, wide), 1) // TILE_SIZE
    grid = jnp.zeros((wide, wide), F32)
    for first in range(tiles):
        for second in range(tiles):
            here = jnp.logical_and(row_in == first, col_in == second)
            grid = jnp.where(here, vv_mask_ref[first, second].astype(F32), grid)
    grid = grid.astype(BF16)
    row_index = virt * share + lax.broadcasted_iota(jnp.int32, (share, wide), 0)
    col_index = lax.broadcasted_iota(jnp.int32, (share, wide), 1)
    pair_mask = over_tiles(row_index, domain) * over_tiles(col_index, domain)
    energy = jnp.broadcast_to(energy_ref[...], (share, wide))
    energy_rows = jnp.sum(jnp.where(col_index == row_index, energy, 0.0), axis=1, keepdims=True)
    denom = energy_rows + energy - occ_i_ref[0] - occ_j_ref[0]
    scale = pair_mask / denom
    loads[7].wait()

    @pl.loop(0, aux)
    def _(q):
        factors[q] = factors[q] * grid

    for first in range(held):
        @pl.when(virt * held + first != integ)
        def _(first=first):
            ov_in = remote(
                ov_mine.at[first], ov_mine.at[first], ov_send.at[0], ov_recv.at[first], virt, integ
            )
            ov_in.wait_recv()
            remote(
                domains.at[first],
                domains.at[first],
                domain_send.at[0],
                domain_recv.at[first],
                virt,
                integ,
            ).wait_recv()

        for source in range(columns):
            @pl.when(jnp.logical_or(virt * held + first != integ, source != virt))
            def _(first=first, source=source):
                landed = pairs.at[first, rows(source)]
                remote(
                    landed,
                    landed,
                    pair_send.at[0],
                    pair_recv.at[first * columns + source],
                    virt,
                    integ,
                ).wait_recv()

    @pl.when(home == virt)
    def _():
        loads[0].wait()

    for first in range(held):
        for upper in range(tiles):
            for lower in range(tiles):
                spot = (
                    first,
                    pl.ds(upper * TILE_SIZE, TILE_SIZE),
                    pl.ds(lower * TILE_SIZE, TILE_SIZE),
                )
                kept = (
                    domains[first, 0:1, pl.ds(upper * TILE_SIZE, TILE_SIZE)]
                    * domains[first, 0:1, pl.ds(lower * TILE_SIZE, TILE_SIZE)]
                ).astype(BF16)
                pairs[spot] = pairs[spot] * kept

    zeta_part = jnp.zeros((aux, wide), F32)
    for first in range(held):
        amps = pairs[first]
        zeta_part += 2.0 * dot_nt(ov_mine[first], amps) - dot_nn(ov_mine[first], amps)
    zetas[virt] = zeta_part

    def zeta_copy(step):
        return remote(
            zetas.at[virt],
            zetas.at[virt],
            zeta_send.at[step],
            zeta_recv.at[virt],
            lax.rem(virt + step, columns),
            integ,
        )

    for step in range(1, columns):
        zeta_copy(step).start()

    near = columns // HALVES
    my_half = virt // near

    def ladder(first, start, depth):
        amps = pairs[first]
        chosen = pl.ds(pl.multiple_of(start, share), depth)

        def add(group, total):
            block = factors[pl.ds(group * GROUP, GROUP)]
            some = factors[pl.ds(group * GROUP, GROUP), chosen]
            weighted = dot_nn(some.reshape(GROUP * depth, wide), amps).astype(BF16)
            for q in range(GROUP):
                total = total + dot_nt(weighted[q * depth:(q + 1) * depth], block[q])
            return total

        return lax.fori_loop(0, aux // GROUP, add, jnp.zeros((depth, wide), F32))

    def cycle(first, start, depth):
        chosen = pl.ds(pl.multiple_of(start, share), depth)
        upper, lower = zeta_rows[0, chosen], zeta_rows[1, chosen]
        return dot_nn(upper, ov_mine[first]) + dot_nn(lower, ov_mine[first])

    def gather_zeta():
        for step in range(1, columns):
            source = lax.rem(virt + step, columns)
            landed = zetas.at[source]
            remote(
                landed, landed, zeta_send.at[0], zeta_recv.at[source], source, integ
            ).wait_recv()
        zeta = zetas[0]
        for column in range(1, columns):
            zeta = zeta + zetas[column]
        zeta = zeta.T
        upper = zeta.astype(BF16)
        zeta_rows[0] = upper
        zeta_rows[1] = (zeta - upper.astype(F32)).astype(BF16)

    def hop_copy(first, row):
        return remote(
            terms.at[first, rows(row)],
            hops.at[virt * held + first],
            hop_send.at[first * columns + row],
            hop_recv.at[virt * held + first],
            row,
            integ,
        )

    def part_copy(which):
        return remote(
            hops.at[which],
            parts.at[integ],
            part_send.at[which],
            part_recv.at[integ],
            virt,
            which,
        )

    def pass_on(which):
        @pl.when(which != integ)
        def _():
            part_copy(which).start()

        @pl.when(which == integ)
        def _():
            parts[integ] = hops[which]

    def work(first):
        other = lax.rem(my_half + 1, HALVES) * near
        chunks = [(other, near)]
        for step in range(1, near + 1):
            chunks.append((my_half * near + lax.rem(virt + step, near), 1))
        for turn, (row, count) in enumerate(chunks):
            total = ladder(first, row * share, count * share)
            if held == 1 and turn == 0:
                gather_zeta()
            total = (total + cycle(first, row * share, count * share)).astype(BF16)
            if turn < near:
                terms[first, pl.ds(pl.multiple_of(row * share, share), count * share)] = total
                for offset in range(count):
                    hop_copy(first, row + offset).start()
            else:
                hops[virt * held + first] = total
                pass_on(virt * held + first)

    if held == 1:
        work(0)
    else:
        gather_zeta()
        pl.loop(0, held)(work)

    for turn in range(HALVES):
        half = lax.rem(my_half + 1 + turn, HALVES)
        for step in range(near):
            source = half * near + lax.rem(virt + 1 + step, near)

            @pl.when(source != virt)
            def _(source=source):
                for first in range(held):
                    which = source * held + first
                    landed = hops.at[which]
                    remote(
                        landed, landed, hop_send.at[0], hop_recv.at[which], source, integ
                    ).wait_recv()
                    pass_on(which)

    for step in range(1, planes):
        source = lax.rem(integ + step, planes)
        landed = parts.at[source]
        remote(
            landed, landed, part_send.at[0], part_recv.at[source], virt, source
        ).wait_recv()

    total = parts[0].astype(F32)
    for source in range(1, planes):
        total = total + parts[source].astype(F32)
    out_ref[0, 0] = (total * scale).astype(BF16)

    for step in range(1, columns):
        zeta_copy(step).wait_send()
    for to_integ in range(planes):
        @pl.when(jnp.logical_or(home != virt, to_integ != integ))
        def _(to_integ=to_integ):
            pair_copy(to_integ).wait_send()

    @pl.when(home == virt)
    def _():
        for step in range(1, planes):
            domain_copy(step).wait_send()
            ov_copy(step).wait_send()

    for first in range(held):
        for step in range(1, columns):
            hop_copy(first, lax.rem(virt + step, columns)).wait_send()
    for step in range(1, planes):
        part_copy(lax.rem(integ + step, planes)).wait_send()


def body(
    columns,
    planes,
    amplitudes,
    vv_factors,
    ov_factors,
    occ_energy_i,
    occ_energy_j,
    virt_energy,
    vv_mask,
    pair_domain,
):
    share, wide = amplitudes.shape[2:]
    aux = vv_factors.shape[0]
    held = planes // columns
    vmem = pl.BlockSpec(memory_space=pltpu.VMEM)
    smem = pltpu.SMEM
    dma = pltpu.SemaphoreType.DMA
    return pl.pallas_call(
        functools.partial(kernel, columns, planes),
        out_shape=pltpu.VMEM(amplitudes.shape, BF16),
        in_specs=[pl.BlockSpec(memory_space=pltpu.HBM)] * 8,
        out_specs=vmem,
        scratch_shapes=[
            pltpu.VMEM((ov_factors.shape[0], wide), BF16),
            smem(occ_energy_i.shape, F32),
            smem(occ_energy_j.shape, F32),
            pltpu.VMEM((1, wide), F32),
            smem(vv_mask.shape, jnp.int32),
            smem(pair_domain.shape, jnp.int32),
            pltpu.VMEM((aux, wide, wide), BF16),
            pltpu.VMEM((held, 8, wide), F32),
            pltpu.VMEM((held, wide, wide), BF16),
            pltpu.VMEM((held, aux, wide), BF16),
            pltpu.VMEM((columns, aux, wide), F32),
            pltpu.VMEM((2, wide, aux), BF16),
            pltpu.VMEM((held, wide, wide), BF16),
            pltpu.VMEM((planes, share, wide), BF16),
            pltpu.VMEM((planes, share, wide), BF16),
            dma((8,)),
            dma((planes,)),
            dma((planes,)),
            dma((planes,)),
            dma((held,)),
            dma((planes,)),
            dma((held,)),
            dma((columns,)),
            dma((columns,)),
            dma((planes,)),
            dma((planes,)),
            dma((planes,)),
            dma((planes,)),
        ],
        compiler_params=pltpu.CompilerParams(
            collective_id=0, has_side_effects=True, vmem_limit_bytes=60 * 1024 * 1024
        ),
        cost_estimate=pl.CostEstimate(
            flops=4 * held * aux * wide**3, bytes_accessed=2 * aux * wide * wide, transcendentals=0
        ),
    )(
        amplitudes,
        ov_factors.reshape(ov_factors.shape[0], wide),
        occ_energy_i,
        occ_energy_j,
        virt_energy.reshape(1, wide),
        vv_mask,
        pair_domain,
        vv_factors,
    )


def solution(mesh):
    placed = (
        P("pair", "integ", "virt", None),
        P("integ", None, None),
        P(None, "integ", None),
        P("pair"),
        P("integ"),
        P(),
        P(),
        P("pair", "integ", None),
    )
    return jax.shard_map(
        functools.partial(body, mesh.shape["virt"], mesh.shape["integ"]),
        mesh=mesh,
        in_specs=placed,
        out_specs=P("pair", "integ", "virt", None),
        check_vma=False,
    )
```

```python
import functools

import jax
import jax.numpy as jnp
from jax import lax
from jax.experimental import pallas as pl
from jax.experimental.pallas import tpu as pltpu
from jax.sharding import PartitionSpec as P

TILE_SIZE = 128
GROUP = 8
HALVES = 2
MESH = pl.DeviceIdType.MESH
F32 = jnp.float32
BF16 = jnp.bfloat16


def dot_nn(left, right):
    return lax.dot_general(left, right, (((1,), (0,)), ((), ())), preferred_element_type=F32)


def dot_nt(left, right):
    return lax.dot_general(left, right, (((1,), (1,)), ((), ())), preferred_element_type=F32)


def over_tiles(index, values):
    picked = jnp.zeros(index.shape, F32)
    for tile, value in enumerate(values):
        picked = jnp.where(index // TILE_SIZE == tile, value, picked)
    return picked


def kernel(
    columns,
    planes,
    amp_hbm,
    ov_hbm,
    occ_i_hbm,
    occ_j_hbm,
    energy_hbm,
    vv_mask_hbm,
    domain_hbm,
    vv_hbm,
    out_ref,
    ov_ref,
    occ_i_ref,
    occ_j_ref,
    energy_ref,
    vv_mask_ref,
    domain_ref,
    factors,
    domains,
    pairs,
    ov_mine,
    zetas,
    zeta_rows,
    terms,
    hops,
    parts,
    load_sem,
    pair_send,
    pair_recv,
    ov_send,
    ov_recv,
    domain_send,
    domain_recv,
    zeta_send,
    zeta_recv,
    hop_send,
    hop_recv,
    part_send,
    part_recv,
):
    pair = lax.axis_index("pair")
    virt = lax.axis_index("virt")
    integ = lax.axis_index("integ")
    share, wide = amp_hbm.shape[2], amp_hbm.shape[3]
    aux = factors.shape[0]
    tiles = wide // TILE_SIZE
    held = planes // columns
    home = integ // held
    slot = integ % held

    def remote(src, dst, send_sem, recv_sem, to_virt, to_integ):
        return pltpu.make_async_remote_copy(
            src_ref=src,
            dst_ref=dst,
            send_sem=send_sem,
            recv_sem=recv_sem,
            device_id=(pair, to_virt, to_integ),
            device_id_type=MESH,
        )

    def rows(which):
        return pl.ds(pl.multiple_of(which * share, share), share)

    loads = [
        pltpu.make_async_copy(src, dst, load_sem.at[which])
        for which, (src, dst) in enumerate(
            (
                (amp_hbm.at[0, 0], pairs.at[slot, rows(virt)]),
                (domain_hbm, domain_ref),
                (ov_hbm, ov_ref),
                (vv_mask_hbm, vv_mask_ref),
                (energy_hbm, energy_ref),
                (occ_i_hbm, occ_i_ref),
                (occ_j_hbm, occ_j_ref),
                (vv_hbm, factors),
            )
        )
    ]
    for load in loads[1:]:
        load.start()

    @pl.when(home == virt)
    def _():
        loads[0].start()

    barrier = pltpu.get_barrier_semaphore()

    def greet(to_virt, to_integ):
        pl.semaphore_signal(
            barrier, inc=1, device_id=(pair, to_virt, to_integ), device_id_type=MESH
        )

    for step in range(1, planes):
        greet(virt, lax.rem(integ + step, planes))
    for step in range(1, columns):
        greet(lax.rem(virt + step, columns), integ)
    for first in range(held):
        @pl.when(virt * held + first != integ)
        def _(first=first):
            for step in range(1, columns):
                greet(lax.rem(virt + step, columns), virt * held + first)

    away = jnp.where(home != virt, planes - 1, 0)
    pl.semaphore_wait(barrier, planes + columns - 2 + away)

    def ov_copy(step):
        to_integ = lax.rem(integ + step, planes)
        return remote(
            ov_ref.at[pl.ds(pl.multiple_of(to_integ * aux, aux), aux)],
            ov_mine.at[integ],
            ov_send.at[step],
            ov_recv.at[integ],
            virt,
            to_integ,
        )

    def pair_copy(to_integ):
        return remote(
            amp_hbm.at[0, 0],
            pairs.at[slot, rows(virt)],
            pair_send.at[to_integ],
            pair_recv.at[slot * columns + virt],
            home,
            to_integ,
        )

    for turn in range(planes):
        to_integ = jnp.where(2 * integ < planes, planes - 1 - turn, turn)

        @pl.when(jnp.logical_or(home != virt, to_integ != integ))
        def _(to_integ=to_integ):
            pair_copy(to_integ).start()

    loads[1].wait()
    domain = [domain_ref[0, 0, tile].astype(F32) for tile in range(tiles)]
    loads[2].wait()

    def domain_copy(step):
        return remote(
            domains.at[slot],
            domains.at[slot],
            domain_send.at[step],
            domain_recv.at[slot],
            virt,
            lax.rem(integ + step, planes),
        )

    @pl.when(home == virt)
    def _():
        for tile in range(tiles):
            domains[slot, :, pl.ds(tile * TILE_SIZE, TILE_SIZE)] = jnp.full(
                (domains.shape[1], TILE_SIZE), domain[tile], F32
            )
        for step in range(1, planes):
            domain_copy(step).start()

    for step in range(1, planes):
        ov_copy(step).start()
    ov_mine[integ] = ov_ref[pl.ds(pl.multiple_of(integ * aux, aux), aux)]

    for load in loads[3:7]:
        load.wait()

    row_in = lax.broadcasted_iota(jnp.int32, (wide, wide), 0) // TILE_SIZE
    col_in = lax.broadcasted_iota(jnp.int32, (wide, wide), 1) // TILE_SIZE
    grid = jnp.zeros((wide, wide), F32)
    for first in range(tiles):
        for second in range(tiles):
            here = jnp.logical_and(row_in == first, col_in == second)
            grid = jnp.where(here, vv_mask_ref[first, second].astype(F32), grid)
    grid = grid.astype(BF16)
    row_index = virt * share + lax.broadcasted_iota(jnp.int32, (share, wide), 0)
    col_index = lax.broadcasted_iota(jnp.int32, (share, wide), 1)
    pair_mask = over_tiles(row_index, domain) * over_tiles(col_index, domain)
    energy = jnp.broadcast_to(energy_ref[...], (share, wide))
    energy_rows = jnp.sum(jnp.where(col_index == row_index, energy, 0.0), axis=1, keepdims=True)
    denom = energy_rows + energy - occ_i_ref[0] - occ_j_ref[0]
    scale = pair_mask / denom
    loads[7].wait()

    @pl.loop(0, aux)
    def _(q):
        factors[q] = factors[q] * grid

    def ov_arrived(which):
        landed = ov_mine.at[which]
        remote(landed, landed, ov_send.at[0], ov_recv.at[which], virt, integ).wait_recv()

    for first in range(held):
        @pl.when(virt * held + first != integ)
        def _(first=first):
            ov_arrived(virt * held + first)
            remote(
                domains.at[first],
                domains.at[first],
                domain_send.at[0],
                domain_recv.at[first],
                virt,
                integ,
            ).wait_recv()

        for source in range(columns):
            @pl.when(jnp.logical_or(virt * held + first != integ, source != virt))
            def _(first=first, source=source):
                landed = pairs.at[first, rows(source)]
                remote(
                    landed,
                    landed,
                    pair_send.at[0],
                    pair_recv.at[first * columns + source],
                    virt,
                    integ,
                ).wait_recv()

    @pl.when(home == virt)
    def _():
        loads[0].wait()

    for first in range(held):
        for upper in range(tiles):
            for lower in range(tiles):
                spot = (
                    first,
                    pl.ds(upper * TILE_SIZE, TILE_SIZE),
                    pl.ds(lower * TILE_SIZE, TILE_SIZE),
                )
                kept = (
                    domains[first, 0:1, pl.ds(upper * TILE_SIZE, TILE_SIZE)]
                    * domains[first, 0:1, pl.ds(lower * TILE_SIZE, TILE_SIZE)]
                ).astype(BF16)
                pairs[spot] = pairs[spot] * kept

    zeta_part = jnp.zeros((aux, wide), F32)
    for first in range(held):
        amps = pairs[first]
        ov_own = ov_mine[virt * held + first]
        zeta_part += 2.0 * dot_nt(ov_own, amps) - dot_nn(ov_own, amps)
    zetas[virt] = zeta_part

    def zeta_copy(step):
        return remote(
            zetas.at[virt],
            zetas.at[virt],
            zeta_send.at[step],
            zeta_recv.at[virt],
            lax.rem(virt + step, columns),
            integ,
        )

    for step in range(1, columns):
        zeta_copy(step).start()

    near = columns // HALVES
    my_half = virt // near

    def ladder(first, start, depth):
        amps = pairs[first]
        chosen = pl.ds(pl.multiple_of(start, share), depth)

        def add(group, total):
            block = factors[pl.ds(group * GROUP, GROUP)]
            some = factors[pl.ds(group * GROUP, GROUP), chosen]
            weighted = dot_nn(some.reshape(GROUP * depth, wide), amps).astype(BF16)
            for q in range(GROUP):
                total = total + dot_nt(weighted[q * depth:(q + 1) * depth], block[q])
            return total

        return lax.fori_loop(0, aux // GROUP, add, jnp.zeros((depth, wide), F32))

    def gather_zeta():
        for step in range(1, columns):
            source = lax.rem(virt + step, columns)
            landed = zetas.at[source]
            remote(
                landed, landed, zeta_send.at[0], zeta_recv.at[source], source, integ
            ).wait_recv()
        zeta = zetas[0]
        for column in range(1, columns):
            zeta = zeta + zetas[column]
        zeta = zeta.T
        upper = zeta.astype(BF16)
        zeta_rows[0] = upper
        zeta_rows[1] = (zeta - upper.astype(F32)).astype(BF16)

    def hop_copy(first, row):
        return remote(
            terms.at[first, rows(row)],
            hops.at[virt * held + first],
            hop_send.at[first * columns + row],
            hop_recv.at[virt * held + first],
            row,
            integ,
        )

    def part_copy(which):
        return remote(
            hops.at[which],
            parts.at[integ],
            part_send.at[which],
            part_recv.at[integ],
            virt,
            which,
        )

    def pass_on(which):
        upper, lower = zeta_rows[0, rows(virt)], zeta_rows[1, rows(virt)]
        cycle = dot_nn(upper, ov_mine[which]) + dot_nn(lower, ov_mine[which])
        hops[which] = (hops[which].astype(F32) + cycle).astype(BF16)

        @pl.when(which != integ)
        def _():
            part_copy(which).start()

        @pl.when(which == integ)
        def _():
            parts[integ] = hops[which]

    def work(first):
        other = lax.rem(my_half + 1, HALVES) * near
        chunks = [(other, near)]
        for step in range(1, near + 1):
            chunks.append((my_half * near + lax.rem(virt + step, near), 1))
        for turn, (row, count) in enumerate(chunks):
            total = ladder(first, row * share, count * share)
            total = total.astype(BF16)
            if turn < near:
                terms[first, pl.ds(pl.multiple_of(row * share, share), count * share)] = total
                for offset in range(count):
                    hop_copy(first, row + offset).start()
            else:
                hops[virt * held + first] = total

    if held == 1:
        work(0)
    else:
        pl.loop(0, held)(work)

    gather_zeta()
    for first in range(held):
        for away in range(1, columns):
            which = lax.rem(virt + away, columns) * held + first

            @pl.when(which != integ)
            def _(which=which):
                ov_arrived(which)

        pass_on(virt * held + first)

    for turn in range(HALVES):
        half = lax.rem(my_half + 1 + turn, HALVES)
        for step in range(near):
            source = half * near + lax.rem(virt + 1 + step, near)

            @pl.when(source != virt)
            def _(source=source):
                for first in range(held):
                    which = source * held + first
                    landed = hops.at[which]
                    remote(
                        landed, landed, hop_send.at[0], hop_recv.at[which], source, integ
                    ).wait_recv()
                    pass_on(which)

    for step in range(1, planes):
        source = lax.rem(integ + step, planes)
        landed = parts.at[source]
        remote(
            landed, landed, part_send.at[0], part_recv.at[source], virt, source
        ).wait_recv()

    total = parts[0].astype(F32)
    for source in range(1, planes):
        total = total + parts[source].astype(F32)
    out_ref[0, 0] = (total * scale).astype(BF16)

    for step in range(1, columns):
        zeta_copy(step).wait_send()
    for to_integ in range(planes):
        @pl.when(jnp.logical_or(home != virt, to_integ != integ))
        def _(to_integ=to_integ):
            pair_copy(to_integ).wait_send()

    @pl.when(home == virt)
    def _():
        for step in range(1, planes):
            domain_copy(step).wait_send()

    for step in range(1, planes):
        ov_copy(step).wait_send()

    for first in range(held):
        for step in range(1, columns):
            hop_copy(first, lax.rem(virt + step, columns)).wait_send()
    for step in range(1, planes):
        part_copy(lax.rem(integ + step, planes)).wait_send()


def body(
    columns,
    planes,
    amplitudes,
    vv_factors,
    ov_factors,
    occ_energy_i,
    occ_energy_j,
    virt_energy,
    vv_mask,
    pair_domain,
):
    share, wide = amplitudes.shape[2:]
    aux = vv_factors.shape[0]
    held = planes // columns
    vmem = pl.BlockSpec(memory_space=pltpu.VMEM)
    smem = pltpu.SMEM
    dma = pltpu.SemaphoreType.DMA
    return pl.pallas_call(
        functools.partial(kernel, columns, planes),
        out_shape=pltpu.VMEM(amplitudes.shape, BF16),
        in_specs=[pl.BlockSpec(memory_space=pltpu.HBM)] * 8,
        out_specs=vmem,
        scratch_shapes=[
            pltpu.VMEM((ov_factors.shape[0], wide), BF16),
            smem(occ_energy_i.shape, F32),
            smem(occ_energy_j.shape, F32),
            pltpu.VMEM((1, wide), F32),
            smem(vv_mask.shape, jnp.int32),
            smem(pair_domain.shape, jnp.int32),
            pltpu.VMEM((aux, wide, wide), BF16),
            pltpu.VMEM((held, 8, wide), F32),
            pltpu.VMEM((held, wide, wide), BF16),
            pltpu.VMEM((planes, aux, wide), BF16),
            pltpu.VMEM((columns, aux, wide), F32),
            pltpu.VMEM((2, wide, aux), BF16),
            pltpu.VMEM((held, wide, wide), BF16),
            pltpu.VMEM((planes, share, wide), BF16),
            pltpu.VMEM((planes, share, wide), BF16),
            dma((8,)),
            dma((planes,)),
            dma((planes,)),
            dma((planes,)),
            dma((planes,)),
            dma((planes,)),
            dma((held,)),
            dma((columns,)),
            dma((columns,)),
            dma((planes,)),
            dma((planes,)),
            dma((planes,)),
            dma((planes,)),
        ],
        compiler_params=pltpu.CompilerParams(
            collective_id=0, has_side_effects=True, vmem_limit_bytes=60 * 1024 * 1024
        ),
        cost_estimate=pl.CostEstimate(
            flops=4 * held * aux * wide**3, bytes_accessed=2 * aux * wide * wide, transcendentals=0
        ),
    )(
        amplitudes,
        ov_factors.reshape(ov_factors.shape[0], wide),
        occ_energy_i,
        occ_energy_j,
        virt_energy.reshape(1, wide),
        vv_mask,
        pair_domain,
        vv_factors,
    )


def solution(mesh):
    placed = (
        P("pair", "integ", "virt", None),
        P("integ", None, None),
        P(None, "integ", None),
        P("pair"),
        P("integ"),
        P(),
        P(),
        P("pair", "integ", None),
    )
    return jax.shard_map(
        functools.partial(body, mesh.shape["virt"], mesh.shape["integ"]),
        mesh=mesh,
        in_specs=placed,
        out_specs=P("pair", "integ", "virt", None),
        check_vma=False,
    )
```

```python
import functools

import jax
import jax.numpy as jnp
from jax import lax
from jax.experimental import pallas as pl
from jax.experimental.pallas import tpu as pltpu
from jax.sharding import PartitionSpec as P

TILE_SIZE = 128
GROUP = 8
HALVES = 2
MESH = pl.DeviceIdType.MESH
F32 = jnp.float32
BF16 = jnp.bfloat16


def dot_nn(left, right):
    return lax.dot_general(left, right, (((1,), (0,)), ((), ())), preferred_element_type=F32)


def dot_nt(left, right):
    return lax.dot_general(left, right, (((1,), (1,)), ((), ())), preferred_element_type=F32)


def over_tiles(index, values):
    picked = jnp.zeros(index.shape, F32)
    for tile, value in enumerate(values):
        picked = jnp.where(index // TILE_SIZE == tile, value, picked)
    return picked


def kernel(
    columns,
    planes,
    amp_hbm,
    ov_hbm,
    occ_i_hbm,
    occ_j_hbm,
    energy_hbm,
    vv_mask_hbm,
    domain_hbm,
    vv_hbm,
    out_ref,
    ov_ref,
    occ_i_ref,
    occ_j_ref,
    energy_ref,
    vv_mask_ref,
    domain_ref,
    factors,
    turned,
    domains,
    pairs,
    ov_mine,
    zetas,
    zeta_rows,
    terms,
    hops,
    parts,
    load_sem,
    pair_send,
    pair_recv,
    ov_send,
    ov_recv,
    domain_send,
    domain_recv,
    zeta_send,
    zeta_recv,
    hop_send,
    hop_recv,
    part_send,
    part_recv,
):
    pair = lax.axis_index("pair")
    virt = lax.axis_index("virt")
    integ = lax.axis_index("integ")
    share, wide = amp_hbm.shape[2], amp_hbm.shape[3]
    aux = factors.shape[0]
    tiles = wide // TILE_SIZE
    held = planes // columns
    home = integ // held
    slot = integ % held

    def remote(src, dst, send_sem, recv_sem, to_virt, to_integ):
        return pltpu.make_async_remote_copy(
            src_ref=src,
            dst_ref=dst,
            send_sem=send_sem,
            recv_sem=recv_sem,
            device_id=(pair, to_virt, to_integ),
            device_id_type=MESH,
        )

    def rows(which):
        return pl.ds(pl.multiple_of(which * share, share), share)

    loads = [
        pltpu.make_async_copy(src, dst, load_sem.at[which])
        for which, (src, dst) in enumerate(
            (
                (amp_hbm.at[0, 0], pairs.at[slot, rows(virt)]),
                (domain_hbm, domain_ref),
                (ov_hbm, ov_ref),
                (vv_mask_hbm, vv_mask_ref),
                (energy_hbm, energy_ref),
                (occ_i_hbm, occ_i_ref),
                (occ_j_hbm, occ_j_ref),
                (vv_hbm, factors),
            )
        )
    ]
    for load in loads[1:]:
        load.start()

    @pl.when(home == virt)
    def _():
        loads[0].start()

    barrier = pltpu.get_barrier_semaphore()

    def greet(to_virt, to_integ):
        pl.semaphore_signal(
            barrier, inc=1, device_id=(pair, to_virt, to_integ), device_id_type=MESH
        )

    for step in range(1, planes):
        greet(virt, lax.rem(integ + step, planes))
    for step in range(1, columns):
        greet(lax.rem(virt + step, columns), integ)
    for first in range(held):
        @pl.when(virt * held + first != integ)
        def _(first=first):
            for step in range(1, columns):
                greet(lax.rem(virt + step, columns), virt * held + first)

    away = jnp.where(home != virt, planes - 1, 0)
    pl.semaphore_wait(barrier, planes + columns - 2 + away)

    def ov_copy(step):
        to_integ = lax.rem(integ + step, planes)
        return remote(
            ov_ref.at[pl.ds(pl.multiple_of(to_integ * aux, aux), aux)],
            ov_mine.at[integ],
            ov_send.at[step],
            ov_recv.at[integ],
            virt,
            to_integ,
        )

    def pair_copy(to_integ):
        return remote(
            amp_hbm.at[0, 0],
            pairs.at[slot, rows(virt)],
            pair_send.at[to_integ],
            pair_recv.at[slot * columns + virt],
            home,
            to_integ,
        )

    for turn in range(planes):
        to_integ = jnp.where(2 * integ < planes, planes - 1 - turn, turn)

        @pl.when(jnp.logical_or(home != virt, to_integ != integ))
        def _(to_integ=to_integ):
            pair_copy(to_integ).start()

    loads[1].wait()
    domain = [domain_ref[0, 0, tile].astype(F32) for tile in range(tiles)]
    loads[2].wait()

    def domain_copy(step):
        return remote(
            domains.at[slot],
            domains.at[slot],
            domain_send.at[step],
            domain_recv.at[slot],
            virt,
            lax.rem(integ + step, planes),
        )

    @pl.when(home == virt)
    def _():
        for tile in range(tiles):
            domains[slot, :, pl.ds(tile * TILE_SIZE, TILE_SIZE)] = jnp.full(
                (domains.shape[1], TILE_SIZE), domain[tile], F32
            )
        for step in range(1, planes):
            domain_copy(step).start()

    for step in range(1, planes):
        ov_copy(step).start()
    ov_mine[integ] = ov_ref[pl.ds(pl.multiple_of(integ * aux, aux), aux)]

    for load in loads[3:7]:
        load.wait()

    row_in = lax.broadcasted_iota(jnp.int32, (wide, wide), 0) // TILE_SIZE
    col_in = lax.broadcasted_iota(jnp.int32, (wide, wide), 1) // TILE_SIZE
    grid = jnp.zeros((wide, wide), F32)
    for first in range(tiles):
        for second in range(tiles):
            here = jnp.logical_and(row_in == first, col_in == second)
            grid = jnp.where(here, vv_mask_ref[first, second].astype(F32), grid)
    grid = grid.astype(BF16)
    row_index = virt * share + lax.broadcasted_iota(jnp.int32, (share, wide), 0)
    col_index = lax.broadcasted_iota(jnp.int32, (share, wide), 1)
    pair_mask = over_tiles(row_index, domain) * over_tiles(col_index, domain)
    energy = jnp.broadcast_to(energy_ref[...], (share, wide))
    energy_rows = jnp.sum(jnp.where(col_index == row_index, energy, 0.0), axis=1, keepdims=True)
    denom = energy_rows + energy - occ_i_ref[0] - occ_j_ref[0]
    scale = pair_mask / denom
    loads[7].wait()

    @pl.loop(0, aux)
    def _(q):
        kept = factors[q] * grid
        factors[q] = kept
        turned[q] = kept.T

    def ov_arrived(which):
        landed = ov_mine.at[which]
        remote(landed, landed, ov_send.at[0], ov_recv.at[which], virt, integ).wait_recv()

    for first in range(held):
        @pl.when(virt * held + first != integ)
        def _(first=first):
            ov_arrived(virt * held + first)
            remote(
                domains.at[first],
                domains.at[first],
                domain_send.at[0],
                domain_recv.at[first],
                virt,
                integ,
            ).wait_recv()

        for source in range(columns):
            @pl.when(jnp.logical_or(virt * held + first != integ, source != virt))
            def _(first=first, source=source):
                landed = pairs.at[first, rows(source)]
                remote(
                    landed,
                    landed,
                    pair_send.at[0],
                    pair_recv.at[first * columns + source],
                    virt,
                    integ,
                ).wait_recv()

    @pl.when(home == virt)
    def _():
        loads[0].wait()

    for first in range(held):
        for upper in range(tiles):
            for lower in range(tiles):
                spot = (
                    first,
                    pl.ds(upper * TILE_SIZE, TILE_SIZE),
                    pl.ds(lower * TILE_SIZE, TILE_SIZE),
                )
                kept = (
                    domains[first, 0:1, pl.ds(upper * TILE_SIZE, TILE_SIZE)]
                    * domains[first, 0:1, pl.ds(lower * TILE_SIZE, TILE_SIZE)]
                ).astype(BF16)
                pairs[spot] = pairs[spot] * kept

    zeta_part = jnp.zeros((aux, wide), F32)
    for first in range(held):
        amps = pairs[first]
        ov_own = ov_mine[virt * held + first]
        zeta_part += 2.0 * dot_nt(ov_own, amps) - dot_nn(ov_own, amps)
    zetas[virt] = zeta_part

    def zeta_copy(step):
        return remote(
            zetas.at[virt],
            zetas.at[virt],
            zeta_send.at[step],
            zeta_recv.at[virt],
            lax.rem(virt + step, columns),
            integ,
        )

    for step in range(1, columns):
        zeta_copy(step).start()

    near = columns // HALVES
    my_half = virt // near

    def ladder(first, start, depth):
        amps = pairs[first]
        chosen = pl.ds(pl.multiple_of(start, share), depth)

        def add(group, total):
            block = turned[pl.ds(group * GROUP, GROUP)]
            some = factors[pl.ds(group * GROUP, GROUP), chosen]
            weighted = dot_nn(some.reshape(GROUP * depth, wide), amps).astype(BF16)
            for q in range(GROUP):
                total = total + dot_nn(weighted[q * depth:(q + 1) * depth], block[q])
            return total

        return lax.fori_loop(0, aux // GROUP, add, jnp.zeros((depth, wide), F32))

    def gather_zeta():
        for step in range(1, columns):
            source = lax.rem(virt + step, columns)
            landed = zetas.at[source]
            remote(
                landed, landed, zeta_send.at[0], zeta_recv.at[source], source, integ
            ).wait_recv()
        zeta = zetas[0]
        for column in range(1, columns):
            zeta = zeta + zetas[column]
        zeta = zeta.T
        upper = zeta.astype(BF16)
        zeta_rows[0] = upper
        zeta_rows[1] = (zeta - upper.astype(F32)).astype(BF16)

    def hop_copy(first, row):
        return remote(
            terms.at[first, rows(row)],
            hops.at[virt * held + first],
            hop_send.at[first * columns + row],
            hop_recv.at[virt * held + first],
            row,
            integ,
        )

    def part_copy(which):
        return remote(
            hops.at[which],
            parts.at[integ],
            part_send.at[which],
            part_recv.at[integ],
            virt,
            which,
        )

    def pass_on(which):
        upper, lower = zeta_rows[0, rows(virt)], zeta_rows[1, rows(virt)]
        cycle = dot_nn(upper, ov_mine[which]) + dot_nn(lower, ov_mine[which])
        hops[which] = (hops[which].astype(F32) + cycle).astype(BF16)

        @pl.when(which != integ)
        def _():
            part_copy(which).start()

        @pl.when(which == integ)
        def _():
            parts[integ] = hops[which]

    def work(first):
        other = lax.rem(my_half + 1, HALVES) * near
        chunks = [(other, near)]
        for step in range(1, near + 1):
            chunks.append((my_half * near + lax.rem(virt + step, near), 1))
        for turn, (row, count) in enumerate(chunks):
            total = ladder(first, row * share, count * share)
            total = total.astype(BF16)
            if turn < near:
                terms[first, pl.ds(pl.multiple_of(row * share, share), count * share)] = total
                for offset in range(count):
                    hop_copy(first, row + offset).start()
            else:
                hops[virt * held + first] = total

    if held == 1:
        work(0)
    else:
        pl.loop(0, held)(work)

    gather_zeta()
    for first in range(held):
        for away in range(1, columns):
            which = lax.rem(virt + away, columns) * held + first

            @pl.when(which != integ)
            def _(which=which):
                ov_arrived(which)

        pass_on(virt * held + first)

    for turn in range(HALVES):
        half = lax.rem(my_half + 1 + turn, HALVES)
        for step in range(near):
            source = half * near + lax.rem(virt + 1 + step, near)

            @pl.when(source != virt)
            def _(source=source):
                for first in range(held):
                    which = source * held + first
                    landed = hops.at[which]
                    remote(
                        landed, landed, hop_send.at[0], hop_recv.at[which], source, integ
                    ).wait_recv()
                    pass_on(which)

    for step in range(1, planes):
        source = lax.rem(integ + step, planes)
        landed = parts.at[source]
        remote(
            landed, landed, part_send.at[0], part_recv.at[source], virt, source
        ).wait_recv()

    total = parts[0].astype(F32)
    for source in range(1, planes):
        total = total + parts[source].astype(F32)
    out_ref[0, 0] = (total * scale).astype(BF16)

    for step in range(1, columns):
        zeta_copy(step).wait_send()
    for to_integ in range(planes):
        @pl.when(jnp.logical_or(home != virt, to_integ != integ))
        def _(to_integ=to_integ):
            pair_copy(to_integ).wait_send()

    @pl.when(home == virt)
    def _():
        for step in range(1, planes):
            domain_copy(step).wait_send()

    for step in range(1, planes):
        ov_copy(step).wait_send()

    for first in range(held):
        for step in range(1, columns):
            hop_copy(first, lax.rem(virt + step, columns)).wait_send()
    for step in range(1, planes):
        part_copy(lax.rem(integ + step, planes)).wait_send()


def body(
    columns,
    planes,
    amplitudes,
    vv_factors,
    ov_factors,
    occ_energy_i,
    occ_energy_j,
    virt_energy,
    vv_mask,
    pair_domain,
):
    share, wide = amplitudes.shape[2:]
    aux = vv_factors.shape[0]
    held = planes // columns
    vmem = pl.BlockSpec(memory_space=pltpu.VMEM)
    smem = pltpu.SMEM
    dma = pltpu.SemaphoreType.DMA
    return pl.pallas_call(
        functools.partial(kernel, columns, planes),
        out_shape=pltpu.VMEM(amplitudes.shape, BF16),
        in_specs=[pl.BlockSpec(memory_space=pltpu.HBM)] * 8,
        out_specs=vmem,
        scratch_shapes=[
            pltpu.VMEM((ov_factors.shape[0], wide), BF16),
            smem(occ_energy_i.shape, F32),
            smem(occ_energy_j.shape, F32),
            pltpu.VMEM((1, wide), F32),
            smem(vv_mask.shape, jnp.int32),
            smem(pair_domain.shape, jnp.int32),
            pltpu.VMEM((aux, wide, wide), BF16),
            pltpu.VMEM((aux, wide, wide), BF16),
            pltpu.VMEM((held, 8, wide), F32),
            pltpu.VMEM((held, wide, wide), BF16),
            pltpu.VMEM((planes, aux, wide), BF16),
            pltpu.VMEM((columns, aux, wide), F32),
            pltpu.VMEM((2, wide, aux), BF16),
            pltpu.VMEM((held, wide, wide), BF16),
            pltpu.VMEM((planes, share, wide), BF16),
            pltpu.VMEM((planes, share, wide), BF16),
            dma((8,)),
            dma((planes,)),
            dma((planes,)),
            dma((planes,)),
            dma((planes,)),
            dma((planes,)),
            dma((held,)),
            dma((columns,)),
            dma((columns,)),
            dma((planes,)),
            dma((planes,)),
            dma((planes,)),
            dma((planes,)),
        ],
        compiler_params=pltpu.CompilerParams(
            collective_id=0, has_side_effects=True, vmem_limit_bytes=60 * 1024 * 1024
        ),
        cost_estimate=pl.CostEstimate(
            flops=4 * held * aux * wide**3, bytes_accessed=2 * aux * wide * wide, transcendentals=0
        ),
    )(
        amplitudes,
        ov_factors.reshape(ov_factors.shape[0], wide),
        occ_energy_i,
        occ_energy_j,
        virt_energy.reshape(1, wide),
        vv_mask,
        pair_domain,
        vv_factors,
    )


def solution(mesh):
    placed = (
        P("pair", "integ", "virt", None),
        P("integ", None, None),
        P(None, "integ", None),
        P("pair"),
        P("integ"),
        P(),
        P(),
        P("pair", "integ", None),
    )
    return jax.shard_map(
        functools.partial(body, mesh.shape["virt"], mesh.shape["integ"]),
        mesh=mesh,
        in_specs=placed,
        out_specs=P("pair", "integ", "virt", None),
        check_vma=False,
    )
```

```python
import functools

import jax
import jax.numpy as jnp
from jax import lax
from jax.experimental import pallas as pl
from jax.experimental.pallas import tpu as pltpu
from jax.sharding import PartitionSpec as P

TILE_SIZE = 128
GROUP = 8
HALVES = 2
MESH = pl.DeviceIdType.MESH
F32 = jnp.float32
BF16 = jnp.bfloat16


def dot_nn(left, right):
    return lax.dot_general(left, right, (((1,), (0,)), ((), ())), preferred_element_type=F32)


def dot_nt(left, right):
    return lax.dot_general(left, right, (((1,), (1,)), ((), ())), preferred_element_type=F32)


def over_tiles(index, values):
    picked = jnp.zeros(index.shape, F32)
    for tile, value in enumerate(values):
        picked = jnp.where(index // TILE_SIZE == tile, value, picked)
    return picked


def kernel(
    columns,
    planes,
    amp_hbm,
    ov_hbm,
    occ_i_hbm,
    occ_j_hbm,
    energy_hbm,
    vv_mask_hbm,
    domain_hbm,
    vv_hbm,
    out_ref,
    ov_ref,
    occ_i_ref,
    occ_j_ref,
    energy_ref,
    vv_mask_ref,
    domain_ref,
    factors,
    turned,
    domains,
    pairs,
    ov_mine,
    zetas,
    zeta_rows,
    terms,
    hops,
    parts,
    load_sem,
    pair_send,
    pair_recv,
    ov_send,
    ov_recv,
    domain_send,
    domain_recv,
    zeta_send,
    zeta_recv,
    hop_send,
    hop_recv,
    part_send,
    part_recv,
):
    pair = lax.axis_index("pair")
    virt = lax.axis_index("virt")
    integ = lax.axis_index("integ")
    share, wide = amp_hbm.shape[2], amp_hbm.shape[3]
    aux = factors.shape[0]
    tiles = wide // TILE_SIZE
    held = planes // columns
    home = integ // held
    slot = integ % held

    def remote(src, dst, send_sem, recv_sem, to_virt, to_integ):
        return pltpu.make_async_remote_copy(
            src_ref=src,
            dst_ref=dst,
            send_sem=send_sem,
            recv_sem=recv_sem,
            device_id=(pair, to_virt, to_integ),
            device_id_type=MESH,
        )

    def rows(which):
        return pl.ds(pl.multiple_of(which * share, share), share)

    loads = [
        pltpu.make_async_copy(src, dst, load_sem.at[which])
        for which, (src, dst) in enumerate(
            (
                (amp_hbm.at[0, 0], pairs.at[slot, rows(virt)]),
                (domain_hbm, domain_ref),
                (ov_hbm, ov_ref),
                (vv_mask_hbm, vv_mask_ref),
                (energy_hbm, energy_ref),
                (occ_i_hbm, occ_i_ref),
                (occ_j_hbm, occ_j_ref),
                (vv_hbm, factors),
            )
        )
    ]

    barrier = pltpu.get_barrier_semaphore()

    def greet(to_virt, to_integ):
        pl.semaphore_signal(
            barrier, inc=1, device_id=(pair, to_virt, to_integ), device_id_type=MESH
        )

    for step in range(1, planes):
        greet(virt, lax.rem(integ + step, planes))
    for step in range(1, columns):
        greet(lax.rem(virt + step, columns), integ)
    for first in range(held):
        @pl.when(virt * held + first != integ)
        def _(first=first):
            for step in range(1, columns):
                greet(lax.rem(virt + step, columns), virt * held + first)

    for load in loads[1:]:
        load.start()

    @pl.when(home == virt)
    def _():
        loads[0].start()

    away = jnp.where(home != virt, planes - 1, 0)
    pl.semaphore_wait(barrier, planes + columns - 2 + away)

    def ov_copy(step):
        to_integ = lax.rem(integ + step, planes)
        return remote(
            ov_ref.at[pl.ds(pl.multiple_of(to_integ * aux, aux), aux)],
            ov_mine.at[integ],
            ov_send.at[step],
            ov_recv.at[integ],
            virt,
            to_integ,
        )

    def pair_copy(to_integ):
        return remote(
            amp_hbm.at[0, 0],
            pairs.at[slot, rows(virt)],
            pair_send.at[to_integ],
            pair_recv.at[slot * columns + virt],
            home,
            to_integ,
        )

    for turn in range(planes):
        to_integ = jnp.where(2 * integ < planes, planes - 1 - turn, turn)

        @pl.when(jnp.logical_or(home != virt, to_integ != integ))
        def _(to_integ=to_integ):
            pair_copy(to_integ).start()

    loads[1].wait()
    domain = [domain_ref[0, 0, tile].astype(F32) for tile in range(tiles)]
    loads[2].wait()

    def domain_copy(step):
        return remote(
            domains.at[slot],
            domains.at[slot],
            domain_send.at[step],
            domain_recv.at[slot],
            virt,
            lax.rem(integ + step, planes),
        )

    @pl.when(home == virt)
    def _():
        for tile in range(tiles):
            domains[slot, :, pl.ds(tile * TILE_SIZE, TILE_SIZE)] = jnp.full(
                (domains.shape[1], TILE_SIZE), domain[tile], F32
            )
        for step in range(1, planes):
            domain_copy(step).start()
            ov_copy(step).start()

    ov_mine[integ] = ov_ref[pl.ds(pl.multiple_of(integ * aux, aux), aux)]

    for load in loads[3:7]:
        load.wait()

    row_in = lax.broadcasted_iota(jnp.int32, (wide, wide), 0) // TILE_SIZE
    col_in = lax.broadcasted_iota(jnp.int32, (wide, wide), 1) // TILE_SIZE
    grid = jnp.zeros((wide, wide), F32)
    for first in range(tiles):
        for second in range(tiles):
            here = jnp.logical_and(row_in == first, col_in == second)
            grid = jnp.where(here, vv_mask_ref[first, second].astype(F32), grid)
    grid = grid.astype(BF16)
    row_index = virt * share + lax.broadcasted_iota(jnp.int32, (share, wide), 0)
    col_index = lax.broadcasted_iota(jnp.int32, (share, wide), 1)
    pair_mask = over_tiles(row_index, domain) * over_tiles(col_index, domain)
    energy = jnp.broadcast_to(energy_ref[...], (share, wide))
    energy_rows = jnp.sum(jnp.where(col_index == row_index, energy, 0.0), axis=1, keepdims=True)
    denom = energy_rows + energy - occ_i_ref[0] - occ_j_ref[0]
    scale = pair_mask / denom
    loads[7].wait()

    @pl.loop(0, aux)
    def _(q):
        kept = factors[q] * grid
        factors[q] = kept
        turned[q] = kept.T

    def ov_arrived(which):
        landed = ov_mine.at[which]
        remote(landed, landed, ov_send.at[0], ov_recv.at[which], virt, integ).wait_recv()

    for first in range(held):
        @pl.when(virt * held + first != integ)
        def _(first=first):
            ov_arrived(virt * held + first)
            remote(
                domains.at[first],
                domains.at[first],
                domain_send.at[0],
                domain_recv.at[first],
                virt,
                integ,
            ).wait_recv()

        for source in range(columns):
            @pl.when(jnp.logical_or(virt * held + first != integ, source != virt))
            def _(first=first, source=source):
                landed = pairs.at[first, rows(source)]
                remote(
                    landed,
                    landed,
                    pair_send.at[0],
                    pair_recv.at[first * columns + source],
                    virt,
                    integ,
                ).wait_recv()

    @pl.when(home == virt)
    def _():
        loads[0].wait()

    @pl.when(home != virt)
    def _():
        for step in range(1, planes):
            ov_copy(step).start()

    for first in range(held):
        for upper in range(tiles):
            for lower in range(tiles):
                spot = (
                    first,
                    pl.ds(upper * TILE_SIZE, TILE_SIZE),
                    pl.ds(lower * TILE_SIZE, TILE_SIZE),
                )
                kept = (
                    domains[first, 0:1, pl.ds(upper * TILE_SIZE, TILE_SIZE)]
                    * domains[first, 0:1, pl.ds(lower * TILE_SIZE, TILE_SIZE)]
                ).astype(BF16)
                pairs[spot] = pairs[spot] * kept

    zeta_part = jnp.zeros((aux, wide), F32)
    for first in range(held):
        amps = pairs[first]
        ov_own = ov_mine[virt * held + first]
        zeta_part += 2.0 * dot_nt(ov_own, amps) - dot_nn(ov_own, amps)
    zetas[virt] = zeta_part

    def zeta_copy(step):
        return remote(
            zetas.at[virt],
            zetas.at[virt],
            zeta_send.at[step],
            zeta_recv.at[virt],
            lax.rem(virt + step, columns),
            integ,
        )

    for step in range(1, columns):
        zeta_copy(step).start()

    near = columns // HALVES
    my_half = virt // near

    def ladder(first, start, depth):
        amps = pairs[first]
        chosen = pl.ds(pl.multiple_of(start, share), depth)

        def add(group, total):
            block = turned[pl.ds(group * GROUP, GROUP)]
            some = factors[pl.ds(group * GROUP, GROUP), chosen]
            weighted = dot_nn(some.reshape(GROUP * depth, wide), amps).astype(BF16)
            for q in range(GROUP):
                total = total + dot_nn(weighted[q * depth:(q + 1) * depth], block[q])
            return total

        return lax.fori_loop(0, aux // GROUP, add, jnp.zeros((depth, wide), F32))

    def gather_zeta():
        for step in range(1, columns):
            source = lax.rem(virt + step, columns)
            landed = zetas.at[source]
            remote(
                landed, landed, zeta_send.at[0], zeta_recv.at[source], source, integ
            ).wait_recv()
        zeta = zetas[0]
        for column in range(1, columns):
            zeta = zeta + zetas[column]
        zeta = zeta.T
        upper = zeta.astype(BF16)
        zeta_rows[0] = upper
        zeta_rows[1] = (zeta - upper.astype(F32)).astype(BF16)

    def hop_copy(first, row):
        return remote(
            terms.at[first, rows(row)],
            hops.at[virt * held + first],
            hop_send.at[first * columns + row],
            hop_recv.at[virt * held + first],
            row,
            integ,
        )

    def part_copy(which):
        return remote(
            hops.at[which],
            parts.at[integ],
            part_send.at[which],
            part_recv.at[integ],
            virt,
            which,
        )

    def pass_on(which):
        upper, lower = zeta_rows[0, rows(virt)], zeta_rows[1, rows(virt)]
        cycle = dot_nn(upper, ov_mine[which]) + dot_nn(lower, ov_mine[which])
        hops[which] = (hops[which].astype(F32) + cycle).astype(BF16)

        @pl.when(which != integ)
        def _():
            part_copy(which).start()

        @pl.when(which == integ)
        def _():
            parts[integ] = hops[which]

    def work(first):
        other = lax.rem(my_half + 1, HALVES) * near
        chunks = [(other, near)]
        for step in range(1, near + 1):
            chunks.append((my_half * near + lax.rem(virt + step, near), 1))
        for turn, (row, count) in enumerate(chunks):
            total = ladder(first, row * share, count * share)
            total = total.astype(BF16)
            if turn < near:
                terms[first, pl.ds(pl.multiple_of(row * share, share), count * share)] = total
                for offset in range(count):
                    hop_copy(first, row + offset).start()
            else:
                hops[virt * held + first] = total

    if held == 1:
        work(0)
    else:
        pl.loop(0, held)(work)

    gather_zeta()
    for first in range(held):
        for away in range(1, columns):
            which = lax.rem(virt + away, columns) * held + first

            @pl.when(which != integ)
            def _(which=which):
                ov_arrived(which)

        pass_on(virt * held + first)

    for turn in range(HALVES):
        half = lax.rem(my_half + 1 + turn, HALVES)
        for step in range(near):
            source = half * near + lax.rem(virt + 1 + step, near)

            @pl.when(source != virt)
            def _(source=source):
                for first in range(held):
                    which = source * held + first
                    landed = hops.at[which]
                    remote(
                        landed, landed, hop_send.at[0], hop_recv.at[which], source, integ
                    ).wait_recv()
                    pass_on(which)

    for step in range(1, planes):
        source = lax.rem(integ + step, planes)
        landed = parts.at[source]
        remote(
            landed, landed, part_send.at[0], part_recv.at[source], virt, source
        ).wait_recv()

    total = parts[0].astype(F32)
    for source in range(1, planes):
        total = total + parts[source].astype(F32)
    out_ref[0, 0] = (total * scale).astype(BF16)

    for step in range(1, columns):
        zeta_copy(step).wait_send()
    for to_integ in range(planes):
        @pl.when(jnp.logical_or(home != virt, to_integ != integ))
        def _(to_integ=to_integ):
            pair_copy(to_integ).wait_send()

    @pl.when(home == virt)
    def _():
        for step in range(1, planes):
            domain_copy(step).wait_send()

    for step in range(1, planes):
        ov_copy(step).wait_send()

    for first in range(held):
        for step in range(1, columns):
            hop_copy(first, lax.rem(virt + step, columns)).wait_send()
    for step in range(1, planes):
        part_copy(lax.rem(integ + step, planes)).wait_send()


def body(
    columns,
    planes,
    amplitudes,
    vv_factors,
    ov_factors,
    occ_energy_i,
    occ_energy_j,
    virt_energy,
    vv_mask,
    pair_domain,
):
    share, wide = amplitudes.shape[2:]
    aux = vv_factors.shape[0]
    held = planes // columns
    vmem = pl.BlockSpec(memory_space=pltpu.VMEM)
    smem = pltpu.SMEM
    dma = pltpu.SemaphoreType.DMA
    return pl.pallas_call(
        functools.partial(kernel, columns, planes),
        out_shape=pltpu.VMEM(amplitudes.shape, BF16),
        in_specs=[pl.BlockSpec(memory_space=pltpu.HBM)] * 8,
        out_specs=vmem,
        scratch_shapes=[
            pltpu.VMEM((ov_factors.shape[0], wide), BF16),
            smem(occ_energy_i.shape, F32),
            smem(occ_energy_j.shape, F32),
            pltpu.VMEM((1, wide), F32),
            smem(vv_mask.shape, jnp.int32),
            smem(pair_domain.shape, jnp.int32),
            pltpu.VMEM((aux, wide, wide), BF16),
            pltpu.VMEM((aux, wide, wide), BF16),
            pltpu.VMEM((held, 8, wide), F32),
            pltpu.VMEM((held, wide, wide), BF16),
            pltpu.VMEM((planes, aux, wide), BF16),
            pltpu.VMEM((columns, aux, wide), F32),
            pltpu.VMEM((2, wide, aux), BF16),
            pltpu.VMEM((held, wide, wide), BF16),
            pltpu.VMEM((planes, share, wide), BF16),
            pltpu.VMEM((planes, share, wide), BF16),
            dma((8,)),
            dma((planes,)),
            dma((planes,)),
            dma((planes,)),
            dma((planes,)),
            dma((planes,)),
            dma((held,)),
            dma((columns,)),
            dma((columns,)),
            dma((planes,)),
            dma((planes,)),
            dma((planes,)),
            dma((planes,)),
        ],
        compiler_params=pltpu.CompilerParams(
            collective_id=0, has_side_effects=True, vmem_limit_bytes=60 * 1024 * 1024
        ),
        cost_estimate=pl.CostEstimate(
            flops=4 * held * aux * wide**3, bytes_accessed=2 * aux * wide * wide, transcendentals=0
        ),
    )(
        amplitudes,
        ov_factors.reshape(ov_factors.shape[0], wide),
        occ_energy_i,
        occ_energy_j,
        virt_energy.reshape(1, wide),
        vv_mask,
        pair_domain,
        vv_factors,
    )


def solution(mesh):
    placed = (
        P("pair", "integ", "virt", None),
        P("integ", None, None),
        P(None, "integ", None),
        P("pair"),
        P("integ"),
        P(),
        P(),
        P("pair", "integ", None),
    )
    return jax.shard_map(
        functools.partial(body, mesh.shape["virt"], mesh.shape["integ"]),
        mesh=mesh,
        in_specs=placed,
        out_specs=P("pair", "integ", "virt", None),
        check_vma=False,
    )
```

```python
import functools

import jax
import jax.numpy as jnp
from jax import lax
from jax.experimental import pallas as pl
from jax.experimental.pallas import tpu as pltpu
from jax.sharding import PartitionSpec as P

TILE_SIZE = 128
GROUP = 16
HALVES = 2
MESH = pl.DeviceIdType.MESH
F32 = jnp.float32
BF16 = jnp.bfloat16


def dot_nn(left, right):
    return lax.dot_general(left, right, (((1,), (0,)), ((), ())), preferred_element_type=F32)


def dot_nt(left, right):
    return lax.dot_general(left, right, (((1,), (1,)), ((), ())), preferred_element_type=F32)


def over_tiles(index, values):
    picked = jnp.zeros(index.shape, F32)
    for tile, value in enumerate(values):
        picked = jnp.where(index // TILE_SIZE == tile, value, picked)
    return picked


def kernel(
    columns,
    planes,
    amp_hbm,
    ov_hbm,
    occ_i_hbm,
    occ_j_hbm,
    energy_hbm,
    vv_mask_hbm,
    domain_hbm,
    vv_hbm,
    out_ref,
    ov_ref,
    occ_i_ref,
    occ_j_ref,
    energy_ref,
    vv_mask_ref,
    domain_ref,
    factors,
    turned,
    domains,
    pairs,
    ov_mine,
    zetas,
    zeta_rows,
    terms,
    hops,
    parts,
    load_sem,
    pair_send,
    pair_recv,
    ov_send,
    ov_recv,
    domain_send,
    domain_recv,
    zeta_send,
    zeta_recv,
    hop_send,
    hop_recv,
    part_send,
    part_recv,
):
    pair = lax.axis_index("pair")
    virt = lax.axis_index("virt")
    integ = lax.axis_index("integ")
    share, wide = amp_hbm.shape[2], amp_hbm.shape[3]
    aux = factors.shape[0]
    tiles = wide // TILE_SIZE
    held = planes // columns
    home = integ // held
    slot = integ % held

    def remote(src, dst, send_sem, recv_sem, to_virt, to_integ):
        return pltpu.make_async_remote_copy(
            src_ref=src,
            dst_ref=dst,
            send_sem=send_sem,
            recv_sem=recv_sem,
            device_id=(pair, to_virt, to_integ),
            device_id_type=MESH,
        )

    def rows(which):
        return pl.ds(pl.multiple_of(which * share, share), share)

    loads = [
        pltpu.make_async_copy(src, dst, load_sem.at[which])
        for which, (src, dst) in enumerate(
            (
                (amp_hbm.at[0, 0], pairs.at[slot, rows(virt)]),
                (domain_hbm, domain_ref),
                (ov_hbm, ov_ref),
                (vv_mask_hbm, vv_mask_ref),
                (energy_hbm, energy_ref),
                (occ_i_hbm, occ_i_ref),
                (occ_j_hbm, occ_j_ref),
                (vv_hbm, factors),
            )
        )
    ]

    barrier = pltpu.get_barrier_semaphore()

    def greet(to_virt, to_integ):
        pl.semaphore_signal(
            barrier, inc=1, device_id=(pair, to_virt, to_integ), device_id_type=MESH
        )

    for step in range(1, planes):
        greet(virt, lax.rem(integ + step, planes))
    for step in range(1, columns):
        greet(lax.rem(virt + step, columns), integ)
    for first in range(held):
        @pl.when(virt * held + first != integ)
        def _(first=first):
            for step in range(1, columns):
                greet(lax.rem(virt + step, columns), virt * held + first)

    for load in loads[1:]:
        load.start()

    @pl.when(home == virt)
    def _():
        loads[0].start()

    away = jnp.where(home != virt, planes - 1, 0)
    pl.semaphore_wait(barrier, planes + columns - 2 + away)

    def ov_copy(step):
        to_integ = lax.rem(integ + step, planes)
        return remote(
            ov_ref.at[pl.ds(pl.multiple_of(to_integ * aux, aux), aux)],
            ov_mine.at[integ],
            ov_send.at[step],
            ov_recv.at[integ],
            virt,
            to_integ,
        )

    def pair_copy(to_integ):
        return remote(
            amp_hbm.at[0, 0],
            pairs.at[slot, rows(virt)],
            pair_send.at[to_integ],
            pair_recv.at[slot * columns + virt],
            home,
            to_integ,
        )

    for turn in range(planes):
        to_integ = jnp.where(2 * integ < planes, planes - 1 - turn, turn)

        @pl.when(jnp.logical_or(home != virt, to_integ != integ))
        def _(to_integ=to_integ):
            pair_copy(to_integ).start()

    loads[1].wait()
    domain = [domain_ref[0, 0, tile].astype(F32) for tile in range(tiles)]
    loads[2].wait()

    def domain_copy(step):
        return remote(
            domains.at[slot],
            domains.at[slot],
            domain_send.at[step],
            domain_recv.at[slot],
            virt,
            lax.rem(integ + step, planes),
        )

    @pl.when(home == virt)
    def _():
        for tile in range(tiles):
            domains[slot, :, pl.ds(tile * TILE_SIZE, TILE_SIZE)] = jnp.full(
                (domains.shape[1], TILE_SIZE), domain[tile], F32
            )
        for step in range(1, planes):
            domain_copy(step).start()
            ov_copy(step).start()

    ov_mine[integ] = ov_ref[pl.ds(pl.multiple_of(integ * aux, aux), aux)]

    for load in loads[3:7]:
        load.wait()

    row_in = lax.broadcasted_iota(jnp.int32, (wide, wide), 0) // TILE_SIZE
    col_in = lax.broadcasted_iota(jnp.int32, (wide, wide), 1) // TILE_SIZE
    grid = jnp.zeros((wide, wide), F32)
    for first in range(tiles):
        for second in range(tiles):
            here = jnp.logical_and(row_in == first, col_in == second)
            grid = jnp.where(here, vv_mask_ref[first, second].astype(F32), grid)
    grid = grid.astype(BF16)
    row_index = virt * share + lax.broadcasted_iota(jnp.int32, (share, wide), 0)
    col_index = lax.broadcasted_iota(jnp.int32, (share, wide), 1)
    pair_mask = over_tiles(row_index, domain) * over_tiles(col_index, domain)
    energy = jnp.broadcast_to(energy_ref[...], (share, wide))
    energy_rows = jnp.sum(jnp.where(col_index == row_index, energy, 0.0), axis=1, keepdims=True)
    denom = energy_rows + energy - occ_i_ref[0] - occ_j_ref[0]
    scale = pair_mask / denom
    loads[7].wait()

    @pl.loop(0, aux)
    def _(q):
        kept = factors[q] * grid
        factors[q] = kept
        turned[q] = kept.T

    def ov_arrived(which):
        landed = ov_mine.at[which]
        remote(landed, landed, ov_send.at[0], ov_recv.at[which], virt, integ).wait_recv()

    for first in range(held):
        @pl.when(virt * held + first != integ)
        def _(first=first):
            ov_arrived(virt * held + first)
            remote(
                domains.at[first],
                domains.at[first],
                domain_send.at[0],
                domain_recv.at[first],
                virt,
                integ,
            ).wait_recv()

        for source in range(columns):
            @pl.when(jnp.logical_or(virt * held + first != integ, source != virt))
            def _(first=first, source=source):
                landed = pairs.at[first, rows(source)]
                remote(
                    landed,
                    landed,
                    pair_send.at[0],
                    pair_recv.at[first * columns + source],
                    virt,
                    integ,
                ).wait_recv()

    @pl.when(home == virt)
    def _():
        loads[0].wait()

    @pl.when(home != virt)
    def _():
        for step in range(1, planes):
            ov_copy(step).start()

    for first in range(held):
        for upper in range(tiles):
            for lower in range(tiles):
                spot = (
                    first,
                    pl.ds(upper * TILE_SIZE, TILE_SIZE),
                    pl.ds(lower * TILE_SIZE, TILE_SIZE),
                )
                kept = (
                    domains[first, 0:1, pl.ds(upper * TILE_SIZE, TILE_SIZE)]
                    * domains[first, 0:1, pl.ds(lower * TILE_SIZE, TILE_SIZE)]
                ).astype(BF16)
                pairs[spot] = pairs[spot] * kept

    zeta_part = jnp.zeros((aux, wide), F32)
    for first in range(held):
        amps = pairs[first]
        ov_own = ov_mine[virt * held + first]
        zeta_part += 2.0 * dot_nt(ov_own, amps) - dot_nn(ov_own, amps)
    zetas[virt] = zeta_part

    def zeta_copy(step):
        return remote(
            zetas.at[virt],
            zetas.at[virt],
            zeta_send.at[step],
            zeta_recv.at[virt],
            lax.rem(virt + step, columns),
            integ,
        )

    for step in range(1, columns):
        zeta_copy(step).start()

    near = columns // HALVES
    my_half = virt // near

    def ladder(first, start, depth):
        amps = pairs[first]
        chosen = pl.ds(pl.multiple_of(start, share), depth)

        def add(group, total):
            block = turned[pl.ds(group * GROUP, GROUP)]
            some = factors[pl.ds(group * GROUP, GROUP), chosen]
            weighted = dot_nn(some.reshape(GROUP * depth, wide), amps).astype(BF16)
            for q in range(GROUP):
                total = total + dot_nn(weighted[q * depth:(q + 1) * depth], block[q])
            return total

        return lax.fori_loop(0, aux // GROUP, add, jnp.zeros((depth, wide), F32))

    def gather_zeta():
        for step in range(1, columns):
            source = lax.rem(virt + step, columns)
            landed = zetas.at[source]
            remote(
                landed, landed, zeta_send.at[0], zeta_recv.at[source], source, integ
            ).wait_recv()
        zeta = zetas[0]
        for column in range(1, columns):
            zeta = zeta + zetas[column]
        zeta = zeta.T
        upper = zeta.astype(BF16)
        zeta_rows[0] = upper
        zeta_rows[1] = (zeta - upper.astype(F32)).astype(BF16)

    def hop_copy(first, row):
        return remote(
            terms.at[first, rows(row)],
            hops.at[virt * held + first],
            hop_send.at[first * columns + row],
            hop_recv.at[virt * held + first],
            row,
            integ,
        )

    def part_copy(which):
        return remote(
            hops.at[which],
            parts.at[integ],
            part_send.at[which],
            part_recv.at[integ],
            virt,
            which,
        )

    def pass_on(which):
        upper, lower = zeta_rows[0, rows(virt)], zeta_rows[1, rows(virt)]
        cycle = dot_nn(upper, ov_mine[which]) + dot_nn(lower, ov_mine[which])
        hops[which] = (hops[which].astype(F32) + cycle).astype(BF16)

        @pl.when(which != integ)
        def _():
            part_copy(which).start()

        @pl.when(which == integ)
        def _():
            parts[integ] = hops[which]

    def work(first):
        other = lax.rem(my_half + 1, HALVES) * near
        chunks = [(other, near)]
        for step in range(1, near + 1):
            chunks.append((my_half * near + lax.rem(virt + step, near), 1))
        for turn, (row, count) in enumerate(chunks):
            total = ladder(first, row * share, count * share)
            total = total.astype(BF16)
            if turn < near:
                terms[first, pl.ds(pl.multiple_of(row * share, share), count * share)] = total
                for offset in range(count):
                    hop_copy(first, row + offset).start()
            else:
                hops[virt * held + first] = total

    if held == 1:
        work(0)
    else:
        pl.loop(0, held)(work)

    gather_zeta()
    for first in range(held):
        for away in range(1, columns):
            which = lax.rem(virt + away, columns) * held + first

            @pl.when(which != integ)
            def _(which=which):
                ov_arrived(which)

        pass_on(virt * held + first)

    for turn in range(HALVES):
        half = lax.rem(my_half + 1 + turn, HALVES)
        for step in range(near):
            source = half * near + lax.rem(virt + 1 + step, near)

            @pl.when(source != virt)
            def _(source=source):
                for first in range(held):
                    which = source * held + first
                    landed = hops.at[which]
                    remote(
                        landed, landed, hop_send.at[0], hop_recv.at[which], source, integ
                    ).wait_recv()
                    pass_on(which)

    for step in range(1, planes):
        source = lax.rem(integ + step, planes)
        landed = parts.at[source]
        remote(
            landed, landed, part_send.at[0], part_recv.at[source], virt, source
        ).wait_recv()

    total = parts[0].astype(F32)
    for source in range(1, planes):
        total = total + parts[source].astype(F32)
    out_ref[0, 0] = (total * scale).astype(BF16)

    for step in range(1, columns):
        zeta_copy(step).wait_send()
    for to_integ in range(planes):
        @pl.when(jnp.logical_or(home != virt, to_integ != integ))
        def _(to_integ=to_integ):
            pair_copy(to_integ).wait_send()

    @pl.when(home == virt)
    def _():
        for step in range(1, planes):
            domain_copy(step).wait_send()

    for step in range(1, planes):
        ov_copy(step).wait_send()

    for first in range(held):
        for step in range(1, columns):
            hop_copy(first, lax.rem(virt + step, columns)).wait_send()
    for step in range(1, planes):
        part_copy(lax.rem(integ + step, planes)).wait_send()


def body(
    columns,
    planes,
    amplitudes,
    vv_factors,
    ov_factors,
    occ_energy_i,
    occ_energy_j,
    virt_energy,
    vv_mask,
    pair_domain,
):
    share, wide = amplitudes.shape[2:]
    aux = vv_factors.shape[0]
    held = planes // columns
    vmem = pl.BlockSpec(memory_space=pltpu.VMEM)
    smem = pltpu.SMEM
    dma = pltpu.SemaphoreType.DMA
    return pl.pallas_call(
        functools.partial(kernel, columns, planes),
        out_shape=pltpu.VMEM(amplitudes.shape, BF16),
        in_specs=[pl.BlockSpec(memory_space=pltpu.HBM)] * 8,
        out_specs=vmem,
        scratch_shapes=[
            pltpu.VMEM((ov_factors.shape[0], wide), BF16),
            smem(occ_energy_i.shape, F32),
            smem(occ_energy_j.shape, F32),
            pltpu.VMEM((1, wide), F32),
            smem(vv_mask.shape, jnp.int32),
            smem(pair_domain.shape, jnp.int32),
            pltpu.VMEM((aux, wide, wide), BF16),
            pltpu.VMEM((aux, wide, wide), BF16),
            pltpu.VMEM((held, 8, wide), F32),
            pltpu.VMEM((held, wide, wide), BF16),
            pltpu.VMEM((planes, aux, wide), BF16),
            pltpu.VMEM((columns, aux, wide), F32),
            pltpu.VMEM((2, wide, aux), BF16),
            pltpu.VMEM((held, wide, wide), BF16),
            pltpu.VMEM((planes, share, wide), BF16),
            pltpu.VMEM((planes, share, wide), BF16),
            dma((8,)),
            dma((planes,)),
            dma((planes,)),
            dma((planes,)),
            dma((planes,)),
            dma((planes,)),
            dma((held,)),
            dma((columns,)),
            dma((columns,)),
            dma((planes,)),
            dma((planes,)),
            dma((planes,)),
            dma((planes,)),
        ],
        compiler_params=pltpu.CompilerParams(
            collective_id=0, has_side_effects=True, vmem_limit_bytes=60 * 1024 * 1024
        ),
        cost_estimate=pl.CostEstimate(
            flops=4 * held * aux * wide**3, bytes_accessed=2 * aux * wide * wide, transcendentals=0
        ),
    )(
        amplitudes,
        ov_factors.reshape(ov_factors.shape[0], wide),
        occ_energy_i,
        occ_energy_j,
        virt_energy.reshape(1, wide),
        vv_mask,
        pair_domain,
        vv_factors,
    )


def solution(mesh):
    placed = (
        P("pair", "integ", "virt", None),
        P("integ", None, None),
        P(None, "integ", None),
        P("pair"),
        P("integ"),
        P(),
        P(),
        P("pair", "integ", None),
    )
    return jax.shard_map(
        functools.partial(body, mesh.shape["virt"], mesh.shape["integ"]),
        mesh=mesh,
        in_specs=placed,
        out_specs=P("pair", "integ", "virt", None),
        check_vma=False,
    )
```

```python
import functools

import jax
import jax.numpy as jnp
from jax import lax
from jax.experimental import pallas as pl
from jax.experimental.pallas import tpu as pltpu
from jax.sharding import PartitionSpec as P

TILE_SIZE = 128
GROUP = 16
HALVES = 2
MESH = pl.DeviceIdType.MESH
F32 = jnp.float32
BF16 = jnp.bfloat16


def dot_nn(left, right):
    return lax.dot_general(left, right, (((1,), (0,)), ((), ())), preferred_element_type=F32)


def dot_nt(left, right):
    return lax.dot_general(left, right, (((1,), (1,)), ((), ())), preferred_element_type=F32)


def over_tiles(index, values):
    picked = jnp.zeros(index.shape, F32)
    for tile, value in enumerate(values):
        picked = jnp.where(index // TILE_SIZE == tile, value, picked)
    return picked


def kernel(
    columns,
    planes,
    amp_hbm,
    ov_hbm,
    occ_i_hbm,
    occ_j_hbm,
    energy_hbm,
    vv_mask_hbm,
    domain_hbm,
    vv_hbm,
    out_ref,
    ov_ref,
    occ_i_ref,
    occ_j_ref,
    energy_ref,
    vv_mask_ref,
    domain_ref,
    factors,
    turned,
    domains,
    pairs,
    ov_mine,
    zetas,
    zeta_rows,
    terms,
    hops,
    parts,
    load_sem,
    pair_send,
    pair_recv,
    ov_send,
    ov_recv,
    domain_send,
    domain_recv,
    zeta_send,
    zeta_recv,
    hop_send,
    hop_recv,
    part_send,
    part_recv,
):
    pair = lax.axis_index("pair")
    virt = lax.axis_index("virt")
    integ = lax.axis_index("integ")
    share, wide = amp_hbm.shape[2], amp_hbm.shape[3]
    aux = factors.shape[0]
    tiles = wide // TILE_SIZE
    held = planes // columns
    home = integ // held
    slot = integ % held

    def remote(src, dst, send_sem, recv_sem, to_virt, to_integ):
        return pltpu.make_async_remote_copy(
            src_ref=src,
            dst_ref=dst,
            send_sem=send_sem,
            recv_sem=recv_sem,
            device_id=(pair, to_virt, to_integ),
            device_id_type=MESH,
        )

    def rows(which):
        return pl.ds(pl.multiple_of(which * share, share), share)

    loads = [
        pltpu.make_async_copy(src, dst, load_sem.at[which])
        for which, (src, dst) in enumerate(
            (
                (amp_hbm.at[0, 0], pairs.at[slot, rows(virt)]),
                (domain_hbm, domain_ref),
                (ov_hbm, ov_ref),
                (vv_mask_hbm, vv_mask_ref),
                (energy_hbm, energy_ref),
                (occ_i_hbm, occ_i_ref),
                (occ_j_hbm, occ_j_ref),
                (vv_hbm, factors),
            )
        )
    ]

    barrier = pltpu.get_barrier_semaphore()

    def greet(to_virt, to_integ):
        pl.semaphore_signal(
            barrier, inc=1, device_id=(pair, to_virt, to_integ), device_id_type=MESH
        )

    for step in range(1, planes):
        greet(virt, lax.rem(integ + step, planes))
    for step in range(1, columns):
        greet(lax.rem(virt + step, columns), integ)
    for first in range(held):
        @pl.when(virt * held + first != integ)
        def _(first=first):
            for step in range(1, columns):
                greet(lax.rem(virt + step, columns), virt * held + first)

    for load in loads[1:]:
        load.start()

    @pl.when(home == virt)
    def _():
        loads[0].start()

    away = jnp.where(home != virt, planes - 1, 0)
    pl.semaphore_wait(barrier, planes + columns - 2 + away)

    def ov_copy(step):
        to_integ = lax.rem(integ + step, planes)
        return remote(
            ov_ref.at[pl.ds(pl.multiple_of(to_integ * aux, aux), aux)],
            ov_mine.at[integ],
            ov_send.at[step],
            ov_recv.at[integ],
            virt,
            to_integ,
        )

    def pair_copy(to_integ):
        return remote(
            amp_hbm.at[0, 0],
            pairs.at[slot, rows(virt)],
            pair_send.at[to_integ],
            pair_recv.at[slot * columns + virt],
            home,
            to_integ,
        )

    for turn in range(planes):
        to_integ = jnp.where(2 * integ < planes, planes - 1 - turn, turn)

        @pl.when(jnp.logical_or(home != virt, to_integ != integ))
        def _(to_integ=to_integ):
            pair_copy(to_integ).start()

    loads[1].wait()
    domain = [domain_ref[0, 0, tile].astype(F32) for tile in range(tiles)]
    loads[2].wait()

    def domain_copy(step):
        return remote(
            domains.at[slot],
            domains.at[slot],
            domain_send.at[step],
            domain_recv.at[slot],
            virt,
            lax.rem(integ + step, planes),
        )

    @pl.when(home == virt)
    def _():
        for tile in range(tiles):
            domains[slot, :, pl.ds(tile * TILE_SIZE, TILE_SIZE)] = jnp.full(
                (domains.shape[1], TILE_SIZE), domain[tile], F32
            )
        for step in range(1, planes):
            domain_copy(step).start()
            ov_copy(step).start()

    ov_mine[integ] = ov_ref[pl.ds(pl.multiple_of(integ * aux, aux), aux)]

    for load in loads[3:7]:
        load.wait()

    row_in = lax.broadcasted_iota(jnp.int32, (wide, wide), 0) // TILE_SIZE
    col_in = lax.broadcasted_iota(jnp.int32, (wide, wide), 1) // TILE_SIZE
    grid = jnp.zeros((wide, wide), F32)
    for first in range(tiles):
        for second in range(tiles):
            here = jnp.logical_and(row_in == first, col_in == second)
            grid = jnp.where(here, vv_mask_ref[first, second].astype(F32), grid)
    grid = grid.astype(BF16)
    row_index = virt * share + lax.broadcasted_iota(jnp.int32, (share, wide), 0)
    col_index = lax.broadcasted_iota(jnp.int32, (share, wide), 1)
    pair_mask = over_tiles(row_index, domain) * over_tiles(col_index, domain)
    energy = jnp.broadcast_to(energy_ref[...], (share, wide))
    energy_rows = jnp.sum(jnp.where(col_index == row_index, energy, 0.0), axis=1, keepdims=True)
    denom = energy_rows + energy - occ_i_ref[0] - occ_j_ref[0]
    scale = pair_mask / denom
    loads[7].wait()

    @pl.loop(0, aux)
    def _(q):
        kept = factors[q] * grid
        factors[q] = kept
        turned[q] = kept.T

    def ov_arrived(which):
        landed = ov_mine.at[which]
        remote(landed, landed, ov_send.at[0], ov_recv.at[which], virt, integ).wait_recv()

    for first in range(held):
        @pl.when(virt * held + first != integ)
        def _(first=first):
            ov_arrived(virt * held + first)
            remote(
                domains.at[first],
                domains.at[first],
                domain_send.at[0],
                domain_recv.at[first],
                virt,
                integ,
            ).wait_recv()

        for source in range(columns):
            @pl.when(jnp.logical_or(virt * held + first != integ, source != virt))
            def _(first=first, source=source):
                landed = pairs.at[first, rows(source)]
                remote(
                    landed,
                    landed,
                    pair_send.at[0],
                    pair_recv.at[first * columns + source],
                    virt,
                    integ,
                ).wait_recv()

    @pl.when(home == virt)
    def _():
        loads[0].wait()

    @pl.when(home != virt)
    def _():
        for step in range(1, planes):
            ov_copy(step).start()

    for first in range(held):
        for upper in range(tiles):
            for lower in range(tiles):
                spot = (
                    first,
                    pl.ds(upper * TILE_SIZE, TILE_SIZE),
                    pl.ds(lower * TILE_SIZE, TILE_SIZE),
                )
                kept = (
                    domains[first, 0:1, pl.ds(upper * TILE_SIZE, TILE_SIZE)]
                    * domains[first, 0:1, pl.ds(lower * TILE_SIZE, TILE_SIZE)]
                ).astype(BF16)
                pairs[spot] = pairs[spot] * kept

    zeta_part = jnp.zeros((aux, wide), F32)
    for first in range(held):
        amps = pairs[first]
        ov_own = ov_mine[virt * held + first]
        zeta_part += 2.0 * dot_nt(ov_own, amps) - dot_nn(ov_own, amps)
    zetas[virt] = zeta_part

    def zeta_copy(step):
        return remote(
            zetas.at[virt],
            zetas.at[virt],
            zeta_send.at[step],
            zeta_recv.at[virt],
            lax.rem(virt + step, columns),
            integ,
        )

    for step in range(1, columns):
        zeta_copy(step).start()

    near = columns // HALVES
    my_half = virt // near

    def ladder(first, start, depth):
        amps = pairs[first]
        chosen = pl.ds(pl.multiple_of(start, share), depth)

        def add(group, total):
            block = turned[pl.ds(group * GROUP, GROUP)]
            some = factors[pl.ds(group * GROUP, GROUP), chosen]
            weighted = dot_nn(some.reshape(GROUP * depth, wide), amps).astype(BF16)
            for q in range(GROUP):
                total = total + dot_nn(weighted[q * depth:(q + 1) * depth], block[q])
            return total

        return lax.fori_loop(0, aux // GROUP, add, jnp.zeros((depth, wide), F32))

    def gather_zeta():
        for step in range(1, columns):
            source = lax.rem(virt + step, columns)
            landed = zetas.at[source]
            remote(
                landed, landed, zeta_send.at[0], zeta_recv.at[source], source, integ
            ).wait_recv()
        zeta = zetas[0]
        for column in range(1, columns):
            zeta = zeta + zetas[column]
        zeta = zeta.T
        upper = zeta.astype(BF16)
        zeta_rows[0] = upper
        zeta_rows[1] = (zeta - upper.astype(F32)).astype(BF16)

    def hop_copy(first, row):
        return remote(
            terms.at[first, rows(row)],
            hops.at[virt * held + first],
            hop_send.at[first * columns + row],
            hop_recv.at[virt * held + first],
            row,
            integ,
        )

    def part_copy(which):
        return remote(
            hops.at[which],
            parts.at[integ],
            part_send.at[which],
            part_recv.at[integ],
            virt,
            which,
        )

    def pass_on(which):
        upper, lower = zeta_rows[0, rows(virt)], zeta_rows[1, rows(virt)]
        cycle = dot_nn(upper, ov_mine[which]) + dot_nn(lower, ov_mine[which])
        hops[which] = (hops[which].astype(F32) + cycle).astype(BF16)

        @pl.when(which != integ)
        def _():
            part_copy(which).start()

        @pl.when(which == integ)
        def _():
            parts[integ] = hops[which]

    def work(first):
        other = lax.rem(my_half + 1, HALVES) * near
        chunks = [(other + offset, 1) for offset in range(near)]
        for step in range(1, near + 1):
            chunks.append((my_half * near + lax.rem(virt + step, near), 1))
        for turn, (row, count) in enumerate(chunks):
            total = ladder(first, row * share, count * share)
            total = total.astype(BF16)
            if turn < len(chunks) - 1:
                terms[first, pl.ds(pl.multiple_of(row * share, share), count * share)] = total
                for offset in range(count):
                    hop_copy(first, row + offset).start()
            else:
                hops[virt * held + first] = total

    if held == 1:
        work(0)
    else:
        pl.loop(0, held)(work)

    gather_zeta()
    for first in range(held):
        for away in range(1, columns):
            which = lax.rem(virt + away, columns) * held + first

            @pl.when(which != integ)
            def _(which=which):
                ov_arrived(which)

        pass_on(virt * held + first)

    for turn in range(HALVES):
        half = lax.rem(my_half + 1 + turn, HALVES)
        for step in range(near):
            source = half * near + lax.rem(virt + 1 + step, near)

            @pl.when(source != virt)
            def _(source=source):
                for first in range(held):
                    which = source * held + first
                    landed = hops.at[which]
                    remote(
                        landed, landed, hop_send.at[0], hop_recv.at[which], source, integ
                    ).wait_recv()
                    pass_on(which)

    for step in range(1, planes):
        source = lax.rem(integ + step, planes)
        landed = parts.at[source]
        remote(
            landed, landed, part_send.at[0], part_recv.at[source], virt, source
        ).wait_recv()

    total = parts[0].astype(F32)
    for source in range(1, planes):
        total = total + parts[source].astype(F32)
    out_ref[0, 0] = (total * scale).astype(BF16)

    for step in range(1, columns):
        zeta_copy(step).wait_send()
    for to_integ in range(planes):
        @pl.when(jnp.logical_or(home != virt, to_integ != integ))
        def _(to_integ=to_integ):
            pair_copy(to_integ).wait_send()

    @pl.when(home == virt)
    def _():
        for step in range(1, planes):
            domain_copy(step).wait_send()

    for step in range(1, planes):
        ov_copy(step).wait_send()

    for first in range(held):
        for step in range(1, columns):
            hop_copy(first, lax.rem(virt + step, columns)).wait_send()
    for step in range(1, planes):
        part_copy(lax.rem(integ + step, planes)).wait_send()


def body(
    columns,
    planes,
    amplitudes,
    vv_factors,
    ov_factors,
    occ_energy_i,
    occ_energy_j,
    virt_energy,
    vv_mask,
    pair_domain,
):
    share, wide = amplitudes.shape[2:]
    aux = vv_factors.shape[0]
    held = planes // columns
    vmem = pl.BlockSpec(memory_space=pltpu.VMEM)
    smem = pltpu.SMEM
    dma = pltpu.SemaphoreType.DMA
    return pl.pallas_call(
        functools.partial(kernel, columns, planes),
        out_shape=pltpu.VMEM(amplitudes.shape, BF16),
        in_specs=[pl.BlockSpec(memory_space=pltpu.HBM)] * 8,
        out_specs=vmem,
        scratch_shapes=[
            pltpu.VMEM((ov_factors.shape[0], wide), BF16),
            smem(occ_energy_i.shape, F32),
            smem(occ_energy_j.shape, F32),
            pltpu.VMEM((1, wide), F32),
            smem(vv_mask.shape, jnp.int32),
            smem(pair_domain.shape, jnp.int32),
            pltpu.VMEM((aux, wide, wide), BF16),
            pltpu.VMEM((aux, wide, wide), BF16),
            pltpu.VMEM((held, 8, wide), F32),
            pltpu.VMEM((held, wide, wide), BF16),
            pltpu.VMEM((planes, aux, wide), BF16),
            pltpu.VMEM((columns, aux, wide), F32),
            pltpu.VMEM((2, wide, aux), BF16),
            pltpu.VMEM((held, wide, wide), BF16),
            pltpu.VMEM((planes, share, wide), BF16),
            pltpu.VMEM((planes, share, wide), BF16),
            dma((8,)),
            dma((planes,)),
            dma((planes,)),
            dma((planes,)),
            dma((planes,)),
            dma((planes,)),
            dma((held,)),
            dma((columns,)),
            dma((columns,)),
            dma((planes,)),
            dma((planes,)),
            dma((planes,)),
            dma((planes,)),
        ],
        compiler_params=pltpu.CompilerParams(
            collective_id=0, has_side_effects=True, vmem_limit_bytes=60 * 1024 * 1024
        ),
        cost_estimate=pl.CostEstimate(
            flops=4 * held * aux * wide**3, bytes_accessed=2 * aux * wide * wide, transcendentals=0
        ),
    )(
        amplitudes,
        ov_factors.reshape(ov_factors.shape[0], wide),
        occ_energy_i,
        occ_energy_j,
        virt_energy.reshape(1, wide),
        vv_mask,
        pair_domain,
        vv_factors,
    )


def solution(mesh):
    placed = (
        P("pair", "integ", "virt", None),
        P("integ", None, None),
        P(None, "integ", None),
        P("pair"),
        P("integ"),
        P(),
        P(),
        P("pair", "integ", None),
    )
    return jax.shard_map(
        functools.partial(body, mesh.shape["virt"], mesh.shape["integ"]),
        mesh=mesh,
        in_specs=placed,
        out_specs=P("pair", "integ", "virt", None),
        check_vma=False,
    )
```
